256 devices in a mesh: enc: 16 (over x, y), blk: 16 (over z, core).
Axes of the slice: x: 4, y: 4, z: 8, core: 2. Of those that a mesh axis runs over, the one named last changes fastest.
Arguments:
- observations: bfloat16 [131072, 128], P(('enc', 'blk')), may hold values from -6 to 6
- lon_index: int32 [256, 512], P(('enc', 'blk')), may hold values from 0 to 1439
- live_count: int32 [256, 256], P(('enc', 'blk')), may hold values from 0 to 2, as said below
- w_in: bfloat16 [128, 512], replicated, may hold values from -0.5 to 0.5
- w_out: bfloat16 [512, 512], replicated, may hold values from -0.25 to 0.25
- w_spec: float32 [256, 512], replicated, may hold values from -4 to 4
- north: float32 [256, 512], P(('enc', 'blk')), may hold values from -0.8 to 0.8
- south: float32 [256, 512], P(('enc', 'blk')), may hold values from -0.8 to 0.8
- w_mix: bfloat16 [512, 512], replicated, may hold values from -0.25 to 0.25
- loss_sensitivity: bfloat16 [256, 1440, 512], P(('enc', 'blk')), may hold values from -6 to 6
Outputs:
- predicted_state: bfloat16 [256, 1440, 512], P(('enc', 'blk'))
- entry_matrix_slope: float32 [128, 512], replicated
- exit_matrix_slope: float32 [512, 512], replicated
- blend_matrix_slope: float32 [512, 512], replicated
- observation_slope: bfloat16 [131072, 128], P(('enc', 'blk'))
The draws below stay inside these ranges and needn't reach their ends.
Inputs may be any that keep to these rules, and one draw needn't show every extreme that they name: In every draw some cycle r has live_count[r, s] = 2 for every source s.
All inputs are finite; a program needn't handle non-finite values.
Results may differ from the reference program's by a relative error of at most 0.0095.
Values may be sent and summed in bfloat16 or wider, within the bound.
No kernel may reach another device: no remote copies, remote signals or barrier semaphores. Data moves between devices by JAX's collectives and lax.ppermute only.
A program may use at most 64 MiB of HBM per device.

```python
import math
import jax
import jax.numpy as jnp
from jax import lax

C = 128
HID = 512
CODE_BREADTH = 512
LON = 1440
MODES = 128
CAP = 2
CYCLES = 256
SLOTS = 512
OBS = 131072


def draw_live_count(key, part):
    key_a, key_b, key_c = jax.random.split(jax.random.fold_in(key, 11), 3)
    cycle_load = jax.random.randint(key_a, (CYCLES, 1), 1, 5)
    drawn = jax.random.randint(key_b, (CYCLES, CYCLES), 0, CAP + 1)
    counts = jnp.minimum(CAP, drawn * cycle_load // 2)
    full_cycle = jax.random.randint(key_c, (), 0, CYCLES)
    forced = jnp.arange(CYCLES, dtype=jnp.int32)[:, None] == full_cycle
    forced = jnp.broadcast_to(forced, (CYCLES, CYCLES))
    return jnp.where(forced, CAP, counts).astype(jnp.int32)


def touch_ends(entries, stream_key, smallest, largest):
    extent = entries.shape
    index_at = [jax.random.randint(jax.random.fold_in(stream_key, axis), (), 0, extent[axis]) for axis in range(len(extent))]
    entries = entries.at[tuple(index_at)].set(smallest)
    longest = extent.index(max(extent))
    index_at[longest] = (index_at[longest] + 1) % extent[longest]
    return entries.at[tuple(index_at)].set(largest)


def steps_of(key, extent, pieces, least, high):
    loudness, own = 1.0, jax.random.fold_in(key, 6)
    for dim, shards_of in pieces:
        heights = jnp.exp(jax.random.uniform(jax.random.fold_in(own, dim), (shards_of,), jnp.float32, least / len(pieces), high / len(pieces)))
        loudness = loudness * jnp.repeat(heights, extent[dim] // shards_of).reshape([-1 if axis == dim else 1 for axis in range(len(extent))])
    return loudness


def centred(key, extent, width, reach, pieces=(), kind=jnp.bfloat16):
    values = width * jax.random.normal(key, extent, jnp.float32)
    if pieces:
        values = values * steps_of(key, extent, pieces, -0.22, 0.18)
    return jnp.clip(values, -reach, reach).astype(kind)


def setup_inputs(seed: int = 0) -> dict:
    key_of = jax.random.split(jax.random.key(seed), 11)
    return {
        "observations": centred(key_of[0], (OBS, C), 1.0, 6.0, ((0, 256),)),
        "lon_index": touch_ends(jax.random.randint(key_of[1], (CYCLES, SLOTS), 0, LON), jax.random.fold_in(key_of[1], 1), 0, LON - 1).astype(jnp.int32),
        "live_count": draw_live_count(jax.random.fold_in(key_of[10], 71), 0),
        "w_in": centred(key_of[3], (C, HID), C ** -0.5, 0.5),
        "w_out": centred(key_of[4], (HID, CODE_BREADTH), HID ** -0.5, 0.25),
        "w_spec": centred(key_of[5], (2 * MODES, CODE_BREADTH), 0.7, 4.0, (), jnp.float32),
        "north": jnp.clip(jax.random.uniform(key_of[6], (CYCLES, CODE_BREADTH), jnp.float32, -0.8, 0.8) * steps_of(key_of[6], (CYCLES, CODE_BREADTH), ((0, 256),), -0.4, 0.0), -0.8, 0.8),
        "south": jnp.clip(jax.random.uniform(key_of[7], (CYCLES, CODE_BREADTH), jnp.float32, -0.8, 0.8) * steps_of(key_of[7], (CYCLES, CODE_BREADTH), ((0, 256),), -0.4, 0.0), -0.8, 0.8),
        "w_mix": centred(key_of[8], (CODE_BREADTH, CODE_BREADTH), CODE_BREADTH ** -0.5, 0.25),
        "loss_sensitivity": centred(key_of[9], (CYCLES, LON, CODE_BREADTH), 1.0, 6.0, ((0, 256),)),
    }


def tables():
    wavenum = jnp.arange(MODES, dtype=jnp.int32)
    lon_pos = jnp.arange(LON, dtype=jnp.int32)
    phases = (wavenum[:, None] * lon_pos[None, :] % LON).astype(jnp.float32) * (2.0 * math.pi / LON)
    forward = jnp.concatenate([jnp.cos(phases), -jnp.sin(phases)], 0).astype(jnp.bfloat16)
    weight = jnp.where(wavenum == 0, 1.0, 2.0).astype(jnp.float32) / LON
    inverse = jnp.concatenate([jnp.cos(phases) * weight[:, None], -jnp.sin(phases) * weight[:, None]], 0).T.astype(jnp.bfloat16)
    return (forward, inverse)

def silu_grad(values):
    logistic = jax.nn.sigmoid(values)
    return logistic * (1.0 + values * (1.0 - logistic))

def cell_table(lon_row, count_row):
    is_live = (jnp.arange(CAP, dtype=jnp.int32)[None, :] < count_row[:, None]).reshape(-1)
    matches = (lon_row[None, :] == jnp.arange(LON, dtype=jnp.int32)[:, None]) & is_live[None, :]
    return (matches.astype(jnp.bfloat16), lax.optimization_barrier(jnp.sum(matches.astype(jnp.float32), axis=1)))

def reference(observations, lon_index, live_count, w_in, w_out, w_spec, north, south, w_mix, loss_sensitivity):
    forward, inverse = tables()
    pre1 = jnp.dot(observations, w_in, preferred_element_type=jnp.float32)
    hidden = jax.nn.silu(pre1).astype(jnp.bfloat16)
    latent = jnp.dot(hidden, w_out, preferred_element_type=jnp.float32).astype(jnp.bfloat16)
    received = latent.reshape(CYCLES, CYCLES, CAP, CODE_BREADTH).transpose(1, 0, 2, 3).reshape(CYCLES, SLOTS, CODE_BREADTH)

    def densify(inputs):
        lat_row, lon_row, count_row = inputs
        onehot, occupancy = cell_table(lon_row, count_row)
        grid_sum = jnp.dot(onehot, lat_row, preferred_element_type=jnp.float32)
        resampled_field = (grid_sum / jnp.maximum(occupancy, 1.0)[:, None]).astype(jnp.bfloat16)
        return (resampled_field, jnp.dot(forward, resampled_field, preferred_element_type=jnp.float32))
    resampled_field, spectrum = lax.map(densify, (received, lon_index, live_count))
    pole_pad = jnp.zeros((1, 2 * MODES, CODE_BREADTH), jnp.float32)
    spec_prev = jnp.concatenate([pole_pad, spectrum[:-1]], 0)
    spec_next = jnp.concatenate([spectrum[1:], pole_pad], 0)
    blended_fourier_modes = (spectrum * w_spec[None] + north[:, None, :] * spec_prev + south[:, None, :] * spec_next).astype(jnp.bfloat16)

    def fourier_operator_apply(running, inputs):
        mix_row, grid_row, grad_out = inputs
        azimuth = jnp.dot(inverse, mix_row, preferred_element_type=jnp.float32).astype(jnp.bfloat16)
        before_nonlinearity = jnp.dot(azimuth, w_mix, preferred_element_type=jnp.float32)
        result = (grid_row.astype(jnp.float32) + jax.nn.silu(before_nonlinearity)).astype(jnp.bfloat16)
        grad_pre = (grad_out.astype(jnp.float32) * silu_grad(before_nonlinearity)).astype(jnp.bfloat16)
        running = running + jnp.dot(azimuth.T, grad_pre, preferred_element_type=jnp.float32)
        grad_az = jnp.dot(grad_pre, w_mix.T, preferred_element_type=jnp.float32).astype(jnp.bfloat16)
        blend_matrix_slope_local = jnp.dot(inverse.T, grad_az, preferred_element_type=jnp.float32)
        return (running, (result, blend_matrix_slope_local))
    blend_matrix_slope_summed, (predicted_state, blend_matrix_slope_local) = lax.scan(fourier_operator_apply, jnp.zeros((CODE_BREADTH, CODE_BREADTH), jnp.float32), (blended_fourier_modes, resampled_field, loss_sensitivity))
    pole_grad = jnp.zeros((1, 2 * MODES, CODE_BREADTH), jnp.float32)
    north_part = north[:, None, :] * blend_matrix_slope_local
    south_part = south[:, None, :] * blend_matrix_slope_local
    from_next = jnp.concatenate([north_part[1:], pole_grad], 0)
    from_prev = jnp.concatenate([pole_grad, south_part[:-1]], 0)
    grad_spec = (w_spec[None] * blend_matrix_slope_local + from_next + from_prev).astype(jnp.bfloat16)

    def backward_cells(inputs):
        spec_row, grad_out, lon_row, count_row = inputs
        onehot, occupancy = cell_table(lon_row, count_row)
        grad_grid = grad_out.astype(jnp.float32) + jnp.dot(forward.T, spec_row, preferred_element_type=jnp.float32)
        scaled = (grad_grid / jnp.maximum(occupancy, 1.0)[:, None]).astype(jnp.bfloat16)
        return jnp.dot(onehot.T, scaled, preferred_element_type=jnp.float32).astype(jnp.bfloat16)
    grad_rows = lax.map(backward_cells, (grad_spec, loss_sensitivity, lon_index, live_count))
    grad_latent = grad_rows.reshape(CYCLES, CYCLES, CAP, CODE_BREADTH).transpose(1, 0, 2, 3).reshape(OBS, CODE_BREADTH)
    observed_factor = 1.0 / math.sqrt(OBS)
    exit_matrix_slope = jnp.dot(hidden.T, grad_latent, preferred_element_type=jnp.float32) * observed_factor
    grad_hidden = jnp.dot(grad_latent, w_out.T, preferred_element_type=jnp.float32)
    grad_pre1 = (grad_hidden * silu_grad(pre1)).astype(jnp.bfloat16)
    entry_matrix_slope = jnp.dot(observations.T, grad_pre1, preferred_element_type=jnp.float32) * observed_factor
    observation_slope = jnp.dot(grad_pre1, w_in.T, preferred_element_type=jnp.float32).astype(jnp.bfloat16)
    blend_matrix_slope = blend_matrix_slope_summed * (1.0 / math.sqrt(CYCLES * LON))
    return (predicted_state, entry_matrix_slope, exit_matrix_slope, blend_matrix_slope, observation_slope)
```

```python
import math

import jax
import jax.numpy as jnp
from jax import lax
from jax.sharding import PartitionSpec as P

LON = 1440
MODES = 128
CAP = 2
BOTH = ("enc", "blk")
BF16 = jnp.bfloat16
F32 = jnp.float32


def dot(a, b):
    return jnp.dot(a, b, preferred_element_type=F32)


def dot_ta(a, b):
    return lax.dot_general(a, b, (((0,), (0,)), ((), ())), preferred_element_type=F32)


def dot_tb(a, b):
    return lax.dot_general(a, b, (((1,), (1,)), ((), ())), preferred_element_type=F32)


def fourier_table():
    wavenum = jnp.arange(MODES, dtype=jnp.int32)
    lon_pos = jnp.arange(LON, dtype=jnp.int32)
    phases = (wavenum[:, None] * lon_pos[None, :] % LON).astype(F32) * (2.0 * math.pi / LON)
    return jnp.concatenate([jnp.cos(phases), -jnp.sin(phases)], 0).astype(BF16)


def silu_grad(values):
    logistic = jax.nn.sigmoid(values)
    return logistic * (1.0 + values * (1.0 - logistic))


def exchange(rows, enc_count, blk_count):
    blocks = rows.reshape(enc_count * blk_count, CAP, rows.shape[-1])
    out = lax.all_to_all(blocks, BOTH, split_axis=0, concat_axis=0, tiled=True)
    return out.reshape(rows.shape)


def neighbour(value, count, step):
    pairs = [(i, i + step) for i in range(count) if 0 <= i + step < count]
    return lax.ppermute(value, BOTH, pairs)


def reduce_all(total, enc_count, blk_count):
    rows, width = total.shape
    half = width // 2
    swap = [(j, j ^ 1) for j in range(blk_count)]
    core = lax.axis_index("blk") % 2
    mine = lax.dynamic_slice(total, (0, core * half), (rows, half))
    other = lax.dynamic_slice(total, (0, (1 - core) * half), (rows, half))
    summed = mine + lax.ppermute(other.astype(BF16), "blk", swap).astype(F32)
    parts = lax.all_to_all(
        summed.astype(BF16).reshape(enc_count, rows // enc_count, half), "enc", split_axis=0, concat_axis=0, tiled=True
    )
    block = jnp.sum(parts.astype(F32), axis=0).astype(BF16)
    step = 2
    while step < blk_count:
        partner = lax.ppermute(block, "blk", [(j, j ^ step) for j in range(blk_count)])
        block = (block.astype(F32) + partner.astype(F32)).astype(BF16)
        step *= 2
    whole = lax.all_to_all(
        jnp.broadcast_to(block[None], (enc_count,) + block.shape), "enc", split_axis=0, concat_axis=0, tiled=True
    ).reshape(rows, half)
    theirs = lax.ppermute(whole, "blk", swap)
    low = jnp.where(core == 0, whole, theirs)
    high = jnp.where(core == 0, theirs, whole)
    return jnp.concatenate([low, high], axis=1).astype(F32)


def shards(
    observations, lon_index, live_count, w_in, w_out, w_spec, north, south, w_mix, loss_sensitivity
):
    enc_count = lax.axis_size("enc")
    blk_count = lax.axis_size("blk")
    devices = enc_count * blk_count
    slots = observations.shape[0]
    rows = exchange(observations, enc_count, blk_count)

    lon = lon_index[0]
    live = (jnp.arange(CAP, dtype=jnp.int32)[None, :] < live_count[0][:, None]).reshape(-1)
    cell = jnp.where(live, lon, -1)
    onehot = (cell[None, :] == jnp.arange(LON, dtype=jnp.int32)[:, None]).astype(BF16)
    shared = jnp.sum((lon[:, None] == cell[None, :]).astype(F32), axis=1)
    share = (1.0 / jnp.maximum(shared, 1.0))[:, None]
    table = fourier_table()
    weight = (jnp.where(jnp.arange(2 * MODES) % MODES == 0, 1.0, 2.0).astype(F32) / LON)[:, None]
    cotangent = loss_sensitivity[0]
    slot_modes = dot(table, onehot).astype(BF16)
    slot_cot = dot_ta(onehot, cotangent).astype(BF16)

    pre1 = dot(rows, w_in)
    hidden = jax.nn.silu(pre1).astype(BF16)
    latent = (dot(hidden, w_out) * share).astype(BF16)
    spectrum = dot(slot_modes, latent)
    sent = spectrum.astype(BF16)
    prev = neighbour(sent, devices, 1).astype(F32)
    following = neighbour(sent, devices, -1).astype(F32)
    mix = (spectrum * w_spec + north * prev + south * following).astype(BF16)
    coeffs = (dot(mix, w_mix) * weight).astype(BF16)
    pre_act = dot_ta(table, coeffs)
    predicted_state = (dot(onehot, latent) + jax.nn.silu(pre_act)).astype(BF16)
    grad_pre = (cotangent.astype(F32) * silu_grad(pre_act)).astype(BF16)
    grad_coeffs = (dot(table, grad_pre) * weight).astype(BF16)
    blend_local = dot_ta(mix, grad_coeffs)
    grad_mix = dot_tb(grad_coeffs, w_mix)
    from_next = neighbour((north * grad_mix).astype(BF16), devices, -1).astype(F32)
    from_prev = neighbour((south * grad_mix).astype(BF16), devices, 1).astype(F32)
    grad_spec = (w_spec * grad_mix + from_next + from_prev).astype(BF16)
    grad_latent = ((slot_cot.astype(F32) + dot_ta(slot_modes, grad_spec)) * share).astype(BF16)
    grad_pre1 = (dot_tb(grad_latent, w_out) * silu_grad(pre1)).astype(BF16)
    row_slope = dot_tb(grad_pre1, w_in).astype(BF16)
    observation_slope = exchange(row_slope, enc_count, blk_count)

    exit_local = dot_ta(hidden, grad_latent)
    entry_local = dot_ta(rows, grad_pre1)
    total = reduce_all(jnp.concatenate([exit_local, blend_local, entry_local], 0), enc_count, blk_count)
    observed_factor = 1.0 / math.sqrt(devices * slots)
    gridding_factor = 1.0 / math.sqrt(devices * LON)
    hid = exit_local.shape[0]
    code = blend_local.shape[0]
    return (
        predicted_state[None],
        total[hid + code :] * observed_factor,
        total[:hid] * observed_factor,
        total[hid : hid + code] * gridding_factor,
        observation_slope,
    )


def solution(mesh):
    placed = (
        P(BOTH, None),
        P(BOTH, None),
        P(BOTH, None),
        P(),
        P(),
        P(),
        P(BOTH, None),
        P(BOTH, None),
        P(),
        P(BOTH, None, None),
    )
    return jax.shard_map(
        shards,
        mesh=mesh,
        in_specs=placed,
        out_specs=(P(BOTH, None, None), P(), P(), P(), P(BOTH, None)),
        check_vma=False,
    )
```

```python
import math

import jax
import jax.numpy as jnp
import numpy as np
from jax import lax
from jax.experimental import pallas as pl
from jax.experimental.pallas import tpu as pltpu
from jax.sharding import PartitionSpec as P

LON = 1440
MODES = 128
CAP = 2
LANES = 128
BOTH = ("enc", "blk")
BF16 = jnp.bfloat16
F32 = jnp.float32
TILES = ((0, 384), (384, 384), (768, 384), (1152, 288))


def dot(a, b):
    return jnp.dot(a, b, preferred_element_type=F32)


def dot_ta(a, b):
    return lax.dot_general(a, b, (((0,), (0,)), ((), ())), preferred_element_type=F32)


def dot_tb(a, b):
    return lax.dot_general(a, b, (((1,), (1,)), ((), ())), preferred_element_type=F32)


def logistic(values):
    return 0.5 * jnp.tanh(0.5 * values) + 0.5


def local_kernel(body, out_shape, flops, moved, *operands, smem=(), room=6):
    vmem = pl.BlockSpec(memory_space=pltpu.VMEM)
    in_specs = [pl.BlockSpec(memory_space=pltpu.SMEM) if i in smem else vmem for i in range(len(operands))]
    single = not isinstance(out_shape, (tuple, list))
    return pl.pallas_call(
        body,
        out_shape=out_shape,
        in_specs=in_specs,
        out_specs=vmem if single else [vmem] * len(out_shape),
        compiler_params=pltpu.CompilerParams(vmem_limit_bytes=room * 1024 * 1024),
        cost_estimate=pl.CostEstimate(flops=flops, bytes_accessed=moved, transcendentals=0),
    )(*operands)


def shape(dims, dtype):
    return jax.ShapeDtypeStruct(dims, dtype)


def mix_body(
    spectrum, prev, following, w_spec, north, south, w_mix, weight, table_t, table, onehot, latent, cotangent,
    state, mix_out, coeffs_out, own, to_prev, to_next,
):
    north_row, south_row = north[...], south[...]
    scale = weight[...]
    mix = (
        spectrum[...] * w_spec[...] + north_row * prev[...].astype(F32) + south_row * following[...].astype(F32)
    ).astype(BF16)
    mix_out[...] = mix
    coeffs = (dot(mix, w_mix[...]) * scale).astype(BF16)
    total = jnp.zeros(spectrum.shape, F32)
    for low, size in TILES:
        part = pl.ds(low, size)
        pre_act = dot(table_t[part, :], coeffs)
        gate = logistic(pre_act)
        silu = pre_act * gate
        state[part, :] = (dot(onehot[part, :], latent[...]) + silu).astype(BF16)
        grad_pre = (cotangent[part, :].astype(F32) * (gate + silu * (1.0 - gate))).astype(BF16)
        total += dot(table[:, part], grad_pre)
    grad_coeffs = (total * scale).astype(BF16)
    coeffs_out[...] = grad_coeffs
    grad_mix = dot_tb(grad_coeffs, w_mix[...])
    own[...] = w_spec[...] * grad_mix
    to_prev[...] = (north_row * grad_mix).astype(BF16)
    to_next[...] = (south_row * grad_mix).astype(BF16)


def back_body(
    core, own, from_next, from_prev, slot_cot, slot_modes, share, w_out, pre1, hidden, rows, w_in, order, mix, coeffs,
    sent, mine, kept,
):
    first = core[0] == 0
    grad_spec = (own[...] + from_next[...].astype(F32) + from_prev[...].astype(F32)).astype(BF16)
    grad_latent = ((slot_cot[...].astype(F32) + dot_ta(slot_modes[...], grad_spec)) * share[...]).astype(BF16)
    gate = logistic(pre1[...])
    slope = gate * (1.0 + pre1[...] * (1.0 - gate))
    grad_pre1 = (dot_tb(grad_latent, w_out[...]) * slope).astype(BF16)
    row_slope = dot_tb(grad_pre1, w_in[...]).astype(BF16)
    ordered = dot(order[...], row_slope).astype(BF16)
    half = ordered.shape[0] // 2
    kept[...] = ordered[:half]
    sent[mine.shape[0] :, :] = ordered[half:]
    at = 0
    depth = mine.shape[0] // 2
    for left, right in ((hidden[...], grad_latent), (mix[...], coeffs[...]), (rows[...], grad_pre1)):
        width = right.shape[1] // 2
        low, high = right[:, :width], right[:, width:]
        near = dot_ta(left, jnp.where(first, low, high))
        far = dot_ta(left, jnp.where(first, high, low)).astype(BF16)
        size = near.shape[0]
        for piece in range(2):
            lanes = slice(piece * LANES, (piece + 1) * LANES)
            mine[piece * depth + at : piece * depth + at + size, :] = near[:, lanes]
            sent[piece * depth + at : piece * depth + at + size, :] = far[:, lanes]
        at += size


def scatter_body(mine, kept, got, out):
    count = out.shape[0]
    size = mine.shape[0] // count
    few = kept.shape[0] // count
    for i in range(count):
        out[i, :few, :] = kept[i * few : (i + 1) * few, :]
        out[i, few : 2 * few, :] = got[mine.shape[0] + i * few : mine.shape[0] + (i + 1) * few, :]
        part = slice(i * size, (i + 1) * size)
        out[i, 2 * few :, :] = (mine[part, :] + got[part, :].astype(F32)).astype(BF16)


def relay_body(got, order, out):
    sources = got.shape[0]
    count = out.shape[0]
    few = order.shape[0] // sources
    more = order.shape[0] // count
    total = got[0, few:, :].astype(F32)
    for i in range(1, sources):
        total += got[i, few:, :].astype(F32)
    total = total.astype(BF16)
    ordered = dot(order[...], jnp.concatenate([got[i, :few, :] for i in range(sources)], 0)).astype(BF16)
    for i in range(count):
        out[i, :more, :] = ordered[i * more : (i + 1) * more, :]
        out[i, more:, :] = total


def gather_body(got, order, out, slope):
    sources = got.shape[0]
    few = order.shape[0] // sources
    total = got[0, few:, :].astype(F32)
    for i in range(1, sources):
        total += got[i, few:, :].astype(F32)
    total = total.astype(BF16)
    for i in range(out.shape[0]):
        out[i, :, :] = total
    ordered = dot(order[...], jnp.concatenate([got[i, :few, :] for i in range(sources)], 0))
    slope[...] = ordered.astype(BF16)


def final_body(factors, core, whole, theirs, entry, exit_, blend):
    first = core[0] == 0
    depth = whole.shape[0] // 2
    for piece in range(2):
        at = piece * depth
        for out, factor in ((exit_, factors[0]), (blend, factors[1]), (entry, factors[0])):
            size = out.shape[0]
            ours = whole[at : at + size, :].astype(F32) * factor
            other = theirs[at : at + size, :].astype(F32) * factor
            out[:, piece * LANES : (piece + 1) * LANES] = jnp.where(first, ours, other)
            out[:, (2 + piece) * LANES : (3 + piece) * LANES] = jnp.where(first, other, ours)
            at += size


def phase_tables():
    product = np.arange(MODES)[:, None] * np.arange(LON)[None, :] % LON
    phases = product.astype(np.float64) * (2.0 * math.pi / LON)
    table = np.concatenate([np.cos(phases), -np.sin(phases)], 0)
    return jnp.asarray(table, BF16), jnp.asarray(np.ascontiguousarray(table.T), BF16)


def selection(source):
    return (source[:, None] == jnp.arange(source.shape[0], dtype=jnp.int32)[None, :]).astype(BF16)


def neighbour(value, count, step):
    pairs = [(i, i + step) for i in range(count) if 0 <= i + step < count]
    return lax.ppermute(value, BOTH, pairs)


def all_swap(blocks, axis, groups=None):
    return lax.all_to_all(blocks, axis, split_axis=0, concat_axis=0, tiled=True, axis_index_groups=groups)


def shards(
    observations, lon_index, live_count, w_in, w_out, w_spec, north, south, w_mix, loss_sensitivity
):
    encs = lax.axis_size("enc")
    blks = lax.axis_size("blk")
    deep = blks // 2
    devices = encs * blks
    slots, channels = observations.shape
    hid, code = w_out.shape
    core = lax.axis_index("blk") % 2
    core_arg = core.astype(jnp.int32).reshape(1)
    swap = [(j, j ^ 1) for j in range(blks)]
    columns = [[2 * i + k for i in range(deep)] for k in range(2)]

    rows = all_swap(observations.reshape(devices, CAP, channels), BOTH).reshape(slots, channels)

    lon = lon_index[0]
    live = (jnp.arange(CAP, dtype=jnp.int32)[None, :] < live_count[0][:, None]).reshape(-1)
    cell = jnp.where(live, lon, -1)
    onehot = (cell[None, :] == jnp.arange(LON, dtype=jnp.int32)[:, None]).astype(BF16)
    shared = jnp.sum((lon[:, None] == cell[None, :]).astype(F32), axis=1)
    share = (1.0 / jnp.maximum(shared, 1.0))[:, None]
    table, table_t = phase_tables()
    weight = jnp.asarray(np.where(np.arange(2 * MODES) % MODES == 0, 1.0, 2.0)[:, None] / LON, F32)
    cotangent = loss_sensitivity[0]
    slot_modes = dot(table, onehot).astype(BF16)
    slot_cot = dot_ta(onehot, cotangent).astype(BF16)
    at = jnp.arange(slots, dtype=jnp.int32)
    slot = at % CAP
    half = slots // 2
    enc_at, z_at = at % half // (deep * CAP), at // CAP % deep
    order1 = selection(((enc_at * deep + z_at) * 2 + (at // half + core) % 2) * CAP + slot)
    z_at, enc_core = at // (encs * 2 * CAP), at // CAP % (encs * 2)
    order2 = selection((enc_core * deep + z_at) * CAP + slot)
    enc_at, z_at, core_at = at // (deep * 2 * CAP), at // (2 * CAP) % deep, at // CAP % 2
    order3 = selection(((z_at * encs + enc_at) * 2 + (core_at + core) % 2) * CAP + slot)

    pre1 = dot(rows, w_in)
    hidden = (pre1 * logistic(pre1)).astype(BF16)
    latent = (dot(hidden, w_out) * share).astype(BF16)
    spectrum = dot(slot_modes, latent)
    outgoing = spectrum.astype(BF16)
    prev = neighbour(outgoing, devices, 1)
    following = neighbour(outgoing, devices, -1)

    modes = (2 * MODES, code)
    state, mix, coeffs, own, to_prev, to_next = local_kernel(
        mix_body,
        [
            shape((LON, code), BF16), shape(modes, BF16), shape(modes, BF16),
            shape(modes, F32), shape(modes, BF16), shape(modes, BF16),
        ],
        2 * LON * code * (4 * MODES + slots),
        8 * LON * code,
        spectrum, prev, following, w_spec, north, south, w_mix, weight, table_t, table, onehot, latent, cotangent,
        room=12,
    )
    from_next = neighbour(to_prev, devices, -1)
    from_prev = neighbour(to_next, devices, 1)
    depth = hid + code + channels
    sent, mine, kept = local_kernel(
        back_body,
        [shape((2 * depth + half, LANES), BF16), shape((2 * depth, LANES), F32), shape((half, LANES), BF16)],
        2 * slots * code * 1500,
        6 * slots * code,
        core_arg, own, from_next, from_prev, slot_cot, slot_modes, share, w_out, pre1, hidden, rows, w_in, order1, mix, coeffs,
        smem=(0,),
        room=10,
    )
    got = lax.ppermute(sent, "blk", swap)
    chunk = 2 * depth // encs
    few, more = slots // encs, slots // deep
    parts = local_kernel(
        scatter_body, shape((encs, few + chunk, LANES), BF16), depth * LANES, 16 * depth * LANES, mine, kept, got
    )
    parts = all_swap(parts, "enc")
    parts = local_kernel(
        relay_body, shape((deep, more + chunk, LANES), BF16), 10 * depth * LANES, 8 * depth * LANES, parts, order2
    )
    parts = all_swap(parts, "blk", columns)
    spread, observation_slope = local_kernel(
        gather_body,
        [shape((encs, chunk, LANES), BF16), shape((slots, LANES), BF16)],
        10 * depth * LANES,
        8 * depth * LANES,
        parts, order3,
    )
    whole = all_swap(spread, "enc").reshape(2 * depth, LANES)
    theirs = lax.ppermute(whole, "blk", swap)
    factors = jnp.array([1.0 / math.sqrt(devices * slots), 1.0 / math.sqrt(devices * LON)], F32)
    entry, exit_, blend = local_kernel(
        final_body,
        [shape((channels, hid), F32), shape((hid, code), F32), shape((code, code), F32)],
        4 * depth * code,
        6 * depth * code,
        factors, core_arg, whole, theirs,
        smem=(0, 1),
    )
    return state[None], entry, exit_, blend, observation_slope


def solution(mesh):
    placed = (
        P(BOTH, None),
        P(BOTH, None),
        P(BOTH, None),
        P(),
        P(),
        P(),
        P(BOTH, None),
        P(BOTH, None),
        P(),
        P(BOTH, None, None),
    )
    return jax.shard_map(
        shards,
        mesh=mesh,
        in_specs=placed,
        out_specs=(P(BOTH, None, None), P(), P(), P(), P(BOTH, None)),
        check_vma=False,
    )
```

```python
import functools
import math

import jax
import jax.numpy as jnp
import numpy as np
from jax import lax
from jax.experimental import pallas as pl
from jax.experimental.pallas import tpu as pltpu
from jax.sharding import PartitionSpec as P

LON = 1440
MODES = 128
CAP = 2
LANES = 128
BOTH = ("enc", "blk")
BF16 = jnp.bfloat16
F32 = jnp.float32
TILES = ((0, 384), (384, 384), (768, 384), (1152, 288))


def dot(a, b):
    return jnp.dot(a, b, preferred_element_type=F32)


def dot_ta(a, b):
    return lax.dot_general(a, b, (((0,), (0,)), ((), ())), preferred_element_type=F32)


def dot_tb(a, b):
    return lax.dot_general(a, b, (((1,), (1,)), ((), ())), preferred_element_type=F32)


def logistic(values):
    return 0.5 * jnp.tanh(0.5 * values) + 0.5


def local_kernel(body, out_shape, flops, moved, *operands, smem=(), hbm=(), hbm_out=(), room=6):
    vmem = pl.BlockSpec(memory_space=pltpu.VMEM)
    far = pl.BlockSpec(memory_space=pltpu.HBM)
    scalar = pl.BlockSpec(memory_space=pltpu.SMEM)
    in_specs = [scalar if i in smem else far if i in hbm else vmem for i in range(len(operands))]
    single = not isinstance(out_shape, (tuple, list))
    copies = len(hbm) + len(hbm_out)
    held = [pltpu.VMEM(operands[i].shape, operands[i].dtype) for i in hbm]
    held += [pltpu.VMEM(out_shape[i].shape, out_shape[i].dtype) for i in hbm_out]
    return pl.pallas_call(
        body,
        out_shape=out_shape,
        in_specs=in_specs,
        out_specs=vmem if single else [far if i in hbm_out else vmem for i in range(len(out_shape))],
        scratch_shapes=held + ([pltpu.SemaphoreType.DMA((copies,))] if copies else []),
        compiler_params=pltpu.CompilerParams(vmem_limit_bytes=room * 1024 * 1024),
        cost_estimate=pl.CostEstimate(flops=flops, bytes_accessed=moved, transcendentals=0),
    )(*operands)


def fetch(sources, held, sems):
    copies = [pltpu.make_async_copy(source, held[i], sems.at[i]) for i, source in enumerate(sources)]
    for copy in copies:
        copy.start()

    def get(i):
        copies[i].wait()
        return held[i][...]

    return get


def shape(dims, dtype):
    return jax.ShapeDtypeStruct(dims, dtype)


def split(index, size):
    assert size & (size - 1) == 0
    return index >> (size.bit_length() - 1), index & (size - 1)


def order_rows(slots, source):
    at = lax.broadcasted_iota(jnp.int32, (slots, 1), 0)
    return (source(at) == lax.broadcasted_iota(jnp.int32, (slots, slots), 1)).astype(BF16)


def mix_body(
    spectrum, prev, following, w_spec, north, south, w_mix, weight, table_t, table, onehot, latent, cotangent,
    state, pair_out, to_prev, to_next, pair, sems,
):
    north_row, south_row = north[...], south[...]
    scale = weight[...]
    mix = (
        spectrum[...] * w_spec[...] + north_row * prev[...].astype(F32) + south_row * following[...].astype(F32)
    ).astype(BF16)
    pair[: mix.shape[0], :] = mix
    coeffs = (dot(mix, w_mix[...]) * scale).astype(BF16)
    total = jnp.zeros(spectrum.shape, F32)
    for low, size in TILES:
        part = pl.ds(low, size)
        pre_act = dot(table_t[part, :], coeffs)
        gate = logistic(pre_act)
        silu = pre_act * gate
        state[part, :] = (dot(onehot[part, :], latent[...]) + silu).astype(BF16)
        grad_pre = (cotangent[part, :].astype(F32) * (gate + silu * (1.0 - gate))).astype(BF16)
        total += dot(table[:, part], grad_pre)
    grad_coeffs = (total * scale).astype(BF16)
    pair[mix.shape[0] :, :] = grad_coeffs
    saved = pltpu.make_async_copy(pair, pair_out, sems.at[0])
    saved.start()
    grad_mix = dot_tb(grad_coeffs, w_mix[...])
    to_prev[...] = (north_row * grad_mix).astype(BF16)
    to_next[...] = (south_row * grad_mix).astype(BF16)
    saved.wait()


def back_body(
    core, from_next, from_prev, share, pair_far, w_mix_far, w_spec_far, rows_far, w_in_far, modes_far, cot_far, w_out_far,
    sent, mine, kept, *held,
):
    get = fetch(
        (pair_far, w_mix_far, w_spec_far, rows_far, w_in_far, modes_far, cot_far, w_out_far), held[:-1], held[-1]
    )
    first = core[0] == 0
    pair = get(0)
    count = pair.shape[0] // 2
    mix, coeffs = pair[:count], pair[count:]
    grad_mix = dot_tb(coeffs, get(1))
    grad_spec = (get(2) * grad_mix + from_next[...].astype(F32) + from_prev[...].astype(F32)).astype(BF16)
    rows, w_in = get(3), get(4)
    pre1 = dot(rows, w_in)
    gate = logistic(pre1)
    hidden = (pre1 * gate).astype(BF16)
    slope = gate * (1.0 + pre1 * (1.0 - gate))
    from_modes = dot_ta(get(5), grad_spec)
    grad_latent = ((get(6).astype(F32) + from_modes) * share[...]).astype(BF16)
    grad_pre1 = (dot_tb(grad_latent, get(7)) * slope).astype(BF16)
    row_slope = dot_tb(grad_pre1, w_in).astype(BF16)
    half = row_slope.shape[0] // 2

    def source(at):
        other, rest = split(at, half)
        block, slot = split(rest, CAP)
        return (block * 2 + ((other + core[0]) & 1)) * CAP + slot

    ordered = dot(order_rows(row_slope.shape[0], source), row_slope).astype(BF16)
    kept[...] = ordered[:half]
    sent[mine.shape[0] :, :] = ordered[half:]
    at = 0
    depth = mine.shape[0] // 2
    for left, right in ((hidden, grad_latent), (mix, coeffs), (rows, grad_pre1)):
        width = right.shape[1] // 2
        low, high = right[:, :width], right[:, width:]
        near = dot_ta(left, jnp.where(first, low, high))
        far = dot_ta(left, jnp.where(first, high, low)).astype(BF16)
        size = near.shape[0]
        for piece in range(2):
            lanes = slice(piece * LANES, (piece + 1) * LANES)
            mine[piece * depth + at : piece * depth + at + size, :] = near[:, lanes]
            sent[piece * depth + at : piece * depth + at + size, :] = far[:, lanes]
        at += size


def scatter_body(mine, kept, got, out):
    count = out.shape[0]
    size = mine.shape[0] // count
    few = kept.shape[0] // count
    for i in range(count):
        out[i, :few, :] = kept[i * few : (i + 1) * few, :]
        out[i, few : 2 * few, :] = got[mine.shape[0] + i * few : mine.shape[0] + (i + 1) * few, :]
        part = slice(i * size, (i + 1) * size)
        out[i, 2 * few :, :] = (mine[part, :] + got[part, :].astype(F32)).astype(BF16)


def relay_body(slots, got, out):
    sources = got.shape[0]
    count = out.shape[0]
    few = slots // sources
    more = slots // count

    def source(at):
        z, rest = split(at, more)
        block, slot = split(rest, CAP)
        return (block * count + z) * CAP + slot

    total = got[0, few:, :].astype(F32)
    for i in range(1, sources):
        total += got[i, few:, :].astype(F32)
    total = total.astype(BF16)
    ordered = dot(order_rows(slots, source), jnp.concatenate([got[i, :few, :] for i in range(sources)], 0)).astype(BF16)
    for i in range(count):
        out[i, :more, :] = ordered[i * more : (i + 1) * more, :]
        out[i, more:, :] = total


def gather_body(core, got, out, slope):
    sources = got.shape[0]
    slots = slope.shape[0]
    few = slots // sources
    encs = out.shape[0]

    def source(at):
        enc, rest = split(at, slots // encs)
        z, rest = split(rest, 2 * CAP)
        which, slot = split(rest, CAP)
        return ((z * encs + enc) * 2 + ((which + core[0]) & 1)) * CAP + slot

    total = got[0, few:, :].astype(F32)
    for i in range(1, sources):
        total += got[i, few:, :].astype(F32)
    total = total.astype(BF16)
    for i in range(out.shape[0]):
        out[i, :, :] = total
    ordered = dot(order_rows(slots, source), jnp.concatenate([got[i, :few, :] for i in range(sources)], 0))
    slope[...] = ordered.astype(BF16)


def final_body(factors, core, whole, theirs, entry, exit_, blend):
    first = core[0] == 0
    depth = whole.shape[0] // 2
    for piece in range(2):
        at = piece * depth
        for out, factor in ((exit_, factors[0]), (blend, factors[1]), (entry, factors[0])):
            size = out.shape[0]
            ours = whole[at : at + size, :].astype(F32) * factor
            other = theirs[at : at + size, :].astype(F32) * factor
            out[:, piece * LANES : (piece + 1) * LANES] = jnp.where(first, ours, other)
            out[:, (2 + piece) * LANES : (3 + piece) * LANES] = jnp.where(first, other, ours)
            at += size


def phase_tables():
    product = np.arange(MODES)[:, None] * np.arange(LON)[None, :] % LON
    phases = product.astype(np.float64) * (2.0 * math.pi / LON)
    table = np.concatenate([np.cos(phases), -np.sin(phases)], 0)
    return jnp.asarray(table, BF16), jnp.asarray(np.ascontiguousarray(table.T), BF16)


def neighbour(value, count, step):
    pairs = [(i, i + step) for i in range(count) if 0 <= i + step < count]
    return lax.ppermute(value, BOTH, pairs)


def all_swap(blocks, axis, groups=None):
    return lax.all_to_all(blocks, axis, split_axis=0, concat_axis=0, tiled=True, axis_index_groups=groups)


def shards(
    observations, lon_index, live_count, w_in, w_out, w_spec, north, south, w_mix, loss_sensitivity
):
    encs = lax.axis_size("enc")
    blks = lax.axis_size("blk")
    deep = blks // 2
    devices = encs * blks
    slots, channels = observations.shape
    hid, code = w_out.shape
    core = lax.axis_index("blk") % 2
    core_arg = core.astype(jnp.int32).reshape(1)
    swap = [(j, j ^ 1) for j in range(blks)]
    columns = [[2 * i + k for i in range(deep)] for k in range(2)]

    rows = all_swap(observations.reshape(devices, CAP, channels), BOTH).reshape(slots, channels)

    lon = lon_index[0]
    live = (jnp.arange(CAP, dtype=jnp.int32)[None, :] < live_count[0][:, None]).reshape(-1)
    cell, core_arg = lax.optimization_barrier((jnp.where(live, lon, -1), core_arg))
    shared = jnp.sum((lon[:, None] == cell[None, :]).astype(F32), axis=1)
    share = (1.0 / jnp.maximum(shared, 1.0))[:, None]
    table, table_t = phase_tables()
    weight = jnp.asarray(np.where(np.arange(2 * MODES) % MODES == 0, 1.0, 2.0)[:, None] / LON, F32)
    cotangent = loss_sensitivity[0]
    half = slots // 2
    modes = (2 * MODES, code)
    onehot = (cell[None, :] == jnp.arange(LON, dtype=jnp.int32)[:, None]).astype(BF16)
    slot_modes = dot(table, onehot).astype(BF16)
    slot_cot = dot_ta(onehot, cotangent).astype(BF16)
    pre1 = dot(rows, w_in)
    hidden = (pre1 * logistic(pre1)).astype(BF16)
    latent = (dot(hidden, w_out) * share).astype(BF16)
    spectrum = dot(slot_modes, latent)
    outgoing = spectrum.astype(BF16)
    prev = neighbour(outgoing, devices, 1)
    following = neighbour(outgoing, devices, -1)

    state, pair, to_prev, to_next = local_kernel(
        mix_body,
        [shape((LON, code), BF16), shape((4 * MODES, code), BF16), shape(modes, BF16), shape(modes, BF16)],
        2 * LON * code * (4 * MODES + slots),
        8 * LON * code,
        spectrum, prev, following, w_spec, north, south, w_mix, weight, table_t, table, onehot, latent, cotangent,
        hbm_out=(1,),
        room=12,
    )
    from_next = neighbour(to_prev, devices, -1)
    from_prev = neighbour(to_next, devices, 1)
    depth = hid + code + channels
    sent, mine, kept = local_kernel(
        back_body,
        [shape((2 * depth + half, LANES), BF16), shape((2 * depth, LANES), F32), shape((half, LANES), BF16)],
        2 * slots * code * 1500,
        6 * slots * code,
        core_arg, from_next, from_prev, share, pair, w_mix, w_spec, rows, w_in, slot_modes, slot_cot, w_out,
        smem=(0,),
        hbm=(4, 5, 6, 7, 8, 9, 10, 11),
        room=16,
    )
    got = lax.ppermute(sent, "blk", swap)
    chunk = 2 * depth // encs
    few, more = slots // encs, slots // deep
    parts = local_kernel(
        scatter_body, shape((encs, few + chunk, LANES), BF16), depth * LANES, 16 * depth * LANES, mine, kept, got
    )
    parts = all_swap(parts, "enc")
    parts = local_kernel(
        functools.partial(relay_body, slots),
        shape((deep, more + chunk, LANES), BF16),
        10 * depth * LANES,
        8 * depth * LANES,
        parts,
    )
    parts = all_swap(parts, "blk", columns)
    spread, observation_slope = local_kernel(
        gather_body,
        [shape((encs, chunk, LANES), BF16), shape((slots, LANES), BF16)],
        10 * depth * LANES,
        8 * depth * LANES,
        core_arg, parts,
        smem=(0,),
    )
    whole = all_swap(spread, "enc").reshape(2 * depth, LANES)
    theirs = lax.ppermute(whole, "blk", swap)
    factors = jnp.array([1.0 / math.sqrt(devices * slots), 1.0 / math.sqrt(devices * LON)], F32)
    entry, exit_, blend = local_kernel(
        final_body,
        [shape((channels, hid), F32), shape((hid, code), F32), shape((code, code), F32)],
        4 * depth * code,
        6 * depth * code,
        factors, core_arg, whole, theirs,
        smem=(0, 1),
    )
    return state[None], entry, exit_, blend, observation_slope


def solution(mesh):
    placed = (
        P(BOTH, None),
        P(BOTH, None),
        P(BOTH, None),
        P(),
        P(),
        P(),
        P(BOTH, None),
        P(BOTH, None),
        P(),
        P(BOTH, None, None),
    )
    return jax.shard_map(
        shards,
        mesh=mesh,
        in_specs=placed,
        out_specs=(P(BOTH, None, None), P(), P(), P(), P(BOTH, None)),
        check_vma=False,
    )
```

```python
import functools
import math

import jax
import jax.numpy as jnp
import numpy as np
from jax import lax
from jax.experimental import pallas as pl
from jax.experimental.pallas import tpu as pltpu
from jax.sharding import PartitionSpec as P

LON = 1440
MODES = 128
CAP = 2
LANES = 128
BOTH = ("enc", "blk")
BF16 = jnp.bfloat16
F32 = jnp.float32
TILES = ((0, 384), (384, 384), (768, 384), (1152, 288))


def dot(a, b):
    return jnp.dot(a, b, preferred_element_type=F32)


def dot_ta(a, b):
    return lax.dot_general(a, b, (((0,), (0,)), ((), ())), preferred_element_type=F32)


def dot_tb(a, b):
    return lax.dot_general(a, b, (((1,), (1,)), ((), ())), preferred_element_type=F32)


def logistic(values):
    return 0.5 * jnp.tanh(0.5 * values) + 0.5


def local_kernel(body, out_shape, flops, moved, *operands, smem=(), room=6, held=(), aliases=None):
    vmem = pl.BlockSpec(memory_space=pltpu.VMEM)
    in_specs = [pl.BlockSpec(memory_space=pltpu.SMEM) if i in smem else vmem for i in range(len(operands))]
    single = not isinstance(out_shape, (tuple, list))
    far = pl.BlockSpec(memory_space=pl.ANY)
    aliases = aliases or {}
    in_specs = [far if i in aliases else spec for i, spec in enumerate(in_specs)]
    out = far if held else vmem
    return pl.pallas_call(
        body,
        out_shape=out_shape,
        in_specs=in_specs,
        out_specs=out if single else [out] * len(out_shape),
        scratch_shapes=[pltpu.VMEM(dims, F32) for dims in held] + ([pltpu.SemaphoreType.DMA((len(held),))] if held else []),
        input_output_aliases=aliases,
        compiler_params=pltpu.CompilerParams(vmem_limit_bytes=room * 1024 * 1024),
        cost_estimate=pl.CostEstimate(flops=flops, bytes_accessed=moved, transcendentals=0),
    )(*operands)


def shape(dims, dtype):
    return jax.ShapeDtypeStruct(dims, dtype)


def split(index, size):
    assert size & (size - 1) == 0
    return index >> (size.bit_length() - 1), index & (size - 1)


def order_rows(slots, source):
    at = lax.broadcasted_iota(jnp.int32, (slots, 1), 0)
    return (source(at) == lax.broadcasted_iota(jnp.int32, (slots, slots), 1)).astype(BF16)


def mix_body(
    spectrum, prev, following, w_spec, north, south, w_mix, weight, table_t, table, cotangent,
    pair, coeffs_out, to_prev, to_next,
):
    north_row, south_row = north[...], south[...]
    scale = weight[...]
    mix = (
        spectrum[...] * w_spec[...] + north_row * prev[...].astype(F32) + south_row * following[...].astype(F32)
    ).astype(BF16)
    pair[: mix.shape[0], :] = mix
    coeffs = (dot(mix, w_mix[...]) * scale).astype(BF16)
    coeffs_out[...] = coeffs
    total = jnp.zeros(spectrum.shape, F32)
    for low, size in TILES:
        part = pl.ds(low, size)
        pre_act = dot(table_t[part, :], coeffs)
        gate = logistic(pre_act)
        slope = gate * (1.0 + pre_act * (1.0 - gate))
        grad_pre = (cotangent[part, :].astype(F32) * slope).astype(BF16)
        total += dot(table[:, part], grad_pre)
    grad_coeffs = (total * scale).astype(BF16)
    pair[mix.shape[0] :, :] = grad_coeffs
    grad_mix = dot_tb(grad_coeffs, w_mix[...])
    to_prev[...] = (north_row * grad_mix).astype(BF16)
    to_next[...] = (south_row * grad_mix).astype(BF16)


def state_body(table_t, coeffs, onehot, latent, state):
    for low, size in TILES:
        part = pl.ds(low, size)
        pre_act = dot(table_t[part, :], coeffs[...])
        state[part, :] = (dot(onehot[part, :], latent[...]) + pre_act * logistic(pre_act)).astype(BF16)


def back_body(
    core, from_next, from_prev, share, pair, w_mix, w_spec, rows, w_in, slot_modes, slot_cot, w_out,
    sent, mine, kept,
):
    first = core[0] == 0
    count = pair.shape[0] // 2
    mix, coeffs = pair[:count, :], pair[count:, :]
    grad_mix = dot_tb(coeffs, w_mix[...])
    grad_spec = (w_spec[...] * grad_mix + from_next[...].astype(F32) + from_prev[...].astype(F32)).astype(BF16)
    pre1 = dot(rows[...], w_in[...])
    gate = logistic(pre1)
    hidden = (pre1 * gate).astype(BF16)
    slope = gate * (1.0 + pre1 * (1.0 - gate))
    from_modes = dot_ta(slot_modes[...], grad_spec)
    grad_latent = ((slot_cot[...].astype(F32) + from_modes) * share[...]).astype(BF16)
    grad_pre1 = (dot_tb(grad_latent, w_out[...]) * slope).astype(BF16)
    row_slope = dot_tb(grad_pre1, w_in[...]).astype(BF16)
    half = row_slope.shape[0] // 2

    def source(at):
        other, rest = split(at, half)
        block, slot = split(rest, CAP)
        return (block * 2 + ((other + core[0]) & 1)) * CAP + slot

    ordered = dot(order_rows(row_slope.shape[0], source), row_slope).astype(BF16)
    kept[...] = ordered[:half]
    sent[mine.shape[0] :, :] = ordered[half:]
    at = 0
    depth = mine.shape[0] // 2
    for left, right in ((hidden, grad_latent), (mix, coeffs), (rows[...], grad_pre1)):
        width = right.shape[1] // 2
        low, high = right[:, :width], right[:, width:]
        near = dot_ta(left, jnp.where(first, low, high))
        far = dot_ta(left, jnp.where(first, high, low)).astype(BF16)
        size = near.shape[0]
        for piece in range(2):
            lanes = slice(piece * LANES, (piece + 1) * LANES)
            mine[piece * depth + at : piece * depth + at + size, :] = near[:, lanes]
            sent[piece * depth + at : piece * depth + at + size, :] = far[:, lanes]
        at += size


def scatter_body(mine, kept, got, out):
    count = out.shape[0]
    size = mine.shape[0] // count
    few = kept.shape[0] // count
    for i in range(count):
        out[i, :few, :] = kept[i * few : (i + 1) * few, :]
        out[i, few : 2 * few, :] = got[mine.shape[0] + i * few : mine.shape[0] + (i + 1) * few, :]
        part = slice(i * size, (i + 1) * size)
        out[i, 2 * few :, :] = (mine[part, :] + got[part, :].astype(F32)).astype(BF16)


def relay_body(slots, got, out):
    sources = got.shape[0]
    count = out.shape[0]
    few = slots // sources
    more = slots // count

    def source(at):
        z, rest = split(at, more)
        block, slot = split(rest, CAP)
        return (block * count + z) * CAP + slot

    total = got[0, few:, :].astype(F32)
    for i in range(1, sources):
        total += got[i, few:, :].astype(F32)
    total = total.astype(BF16)
    ordered = dot(order_rows(slots, source), jnp.concatenate([got[i, :few, :] for i in range(sources)], 0)).astype(BF16)
    for i in range(count):
        out[i, :more, :] = ordered[i * more : (i + 1) * more, :]
        out[i, more:, :] = total


def spread_body(few, got, out):
    total = got[0, few:, :].astype(F32)
    for i in range(1, got.shape[0]):
        total += got[i, few:, :].astype(F32)
    total = total.astype(BF16)
    for i in range(out.shape[0]):
        out[i, :, :] = total


def return_body(encs, core, got, slope):
    sources = got.shape[0]
    slots = slope.shape[0]
    few = slots // sources

    def source(at):
        enc, rest = split(at, slots // encs)
        z, rest = split(rest, 2 * CAP)
        which, slot = split(rest, CAP)
        return ((z * encs + enc) * 2 + ((which + core[0]) & 1)) * CAP + slot

    ordered = dot(order_rows(slots, source), jnp.concatenate([got[i, :few, :] for i in range(sources)], 0))
    slope[...] = ordered.astype(BF16)


def final_body(other, factors, core, half, *refs):
    outs, held, sems = refs[-7:-4], refs[-4:-1], refs[-1]
    side = (core[0] + 1) & 1 if other else core[0]
    width = held[0].shape[1]
    pieces = width // LANES
    depth = half.shape[0] // pieces
    at = 0
    copies = []
    for i, index in enumerate((1, 2, 0)):
        size = held[index].shape[0]
        for piece in range(pieces):
            part = slice(piece * depth + at, piece * depth + at + size)
            held[index][:, piece * LANES : (piece + 1) * LANES] = half[part, :].astype(F32) * factors[i & 1]
        at += size
        target = outs[index].at[:, pl.ds(pl.multiple_of(side * width, width), width)]
        copies.append(pltpu.make_async_copy(held[index], target, sems.at[index]))
        copies[-1].start()
    for copy in copies:
        copy.wait()


def phase_tables():
    product = np.arange(MODES)[:, None] * np.arange(LON)[None, :] % LON
    phases = product.astype(np.float64) * (2.0 * math.pi / LON)
    table = np.concatenate([np.cos(phases), -np.sin(phases)], 0)
    return jnp.asarray(table, BF16), jnp.asarray(np.ascontiguousarray(table.T), BF16)


def neighbour(value, count, step):
    pairs = [(i, i + step) for i in range(count) if 0 <= i + step < count]
    return lax.ppermute(value, BOTH, pairs)


def all_swap(blocks, axis, groups=None):
    return lax.all_to_all(blocks, axis, split_axis=0, concat_axis=0, tiled=True, axis_index_groups=groups)


def shards(
    observations, lon_index, live_count, w_in, w_out, w_spec, north, south, w_mix, loss_sensitivity
):
    encs = lax.axis_size("enc")
    blks = lax.axis_size("blk")
    deep = blks // 2
    devices = encs * blks
    slots, channels = observations.shape
    hid, code = w_out.shape
    core = lax.axis_index("blk") % 2
    core_arg = core.astype(jnp.int32).reshape(1)
    swap = [(j, j ^ 1) for j in range(blks)]
    columns = [[2 * i + k for i in range(deep)] for k in range(2)]

    rows = all_swap(observations.reshape(devices, CAP, channels), BOTH).reshape(slots, channels)

    lon = lon_index[0]
    live = (jnp.arange(CAP, dtype=jnp.int32)[None, :] < live_count[0][:, None]).reshape(-1)
    cell, core_arg = lax.optimization_barrier((jnp.where(live, lon, -1), core_arg))
    shared = jnp.sum((lon[:, None] == cell[None, :]).astype(F32), axis=1)
    share = (1.0 / jnp.maximum(shared, 1.0))[:, None]
    table, table_t = phase_tables()
    weight = jnp.asarray(np.where(np.arange(2 * MODES) % MODES == 0, 1.0, 2.0)[:, None] / LON, F32)
    cotangent = loss_sensitivity[0]
    half = slots // 2
    modes = (2 * MODES, code)
    onehot = (cell[None, :] == jnp.arange(LON, dtype=jnp.int32)[:, None]).astype(BF16)
    slot_modes = dot(table, onehot).astype(BF16)
    slot_cot = dot_ta(onehot, cotangent).astype(BF16)
    pre1 = dot(rows, w_in)
    hidden = (pre1 * logistic(pre1)).astype(BF16)
    latent = (dot(hidden, w_out) * share).astype(BF16)
    spectrum = dot(slot_modes, latent)
    outgoing = spectrum.astype(BF16)
    prev = neighbour(outgoing, devices, 1)
    following = neighbour(outgoing, devices, -1)

    pair, coeffs, to_prev, to_next = local_kernel(
        mix_body,
        [shape((4 * MODES, code), BF16), shape(modes, BF16), shape(modes, BF16), shape(modes, BF16)],
        2 * LON * code * 4 * MODES,
        6 * LON * code,
        spectrum, prev, following, w_spec, north, south, w_mix, weight, table_t, table, cotangent,
        room=12,
    )
    state = local_kernel(
        state_body,
        shape((LON, code), BF16),
        2 * LON * code * (2 * MODES + slots),
        6 * LON * code,
        table_t, coeffs, onehot, latent,
        room=8,
    )
    from_next = neighbour(to_prev, devices, -1)
    from_prev = neighbour(to_next, devices, 1)
    state, pair = lax.optimization_barrier((state, pair))
    depth = hid + code + channels
    sent, mine, kept = local_kernel(
        back_body,
        [shape((2 * depth + half, LANES), BF16), shape((2 * depth, LANES), F32), shape((half, LANES), BF16)],
        2 * slots * code * 1500,
        6 * slots * code,
        core_arg, from_next, from_prev, share, pair, w_mix, w_spec, rows, w_in, slot_modes, slot_cot, w_out,
        smem=(0,),
        room=12,
    )
    got = lax.ppermute(sent, "blk", swap)
    chunk = 2 * depth // encs
    few, more = slots // encs, slots // deep
    parts = local_kernel(
        scatter_body, shape((encs, few + chunk, LANES), BF16), depth * LANES, 16 * depth * LANES, mine, kept, got
    )
    parts = all_swap(parts, "enc")
    parts = local_kernel(
        functools.partial(relay_body, slots),
        shape((deep, more + chunk, LANES), BF16),
        10 * depth * LANES,
        8 * depth * LANES,
        parts,
    )
    parts = all_swap(parts, "blk", columns)
    spread = local_kernel(
        functools.partial(spread_body, more), shape((encs, chunk, LANES), BF16), 10 * depth * LANES, 8 * depth * LANES, parts
    )
    observation_slope = local_kernel(
        functools.partial(return_body, encs),
        shape((slots, LANES), BF16),
        2 * slots * slots * LANES,
        4 * slots * LANES,
        core_arg, parts,
        smem=(0,),
    )
    whole = all_swap(spread, "enc").reshape(2 * depth, LANES)
    theirs = lax.ppermute(whole, "blk", swap)
    factors = jnp.array([1.0 / math.sqrt(devices * slots), 1.0 / math.sqrt(devices * LON)], F32)
    sizes = ((channels, hid), (hid, code), (code, code))
    outs = []
    for other, half_rows in ((False, whole), (True, theirs)):
        outs = local_kernel(
            functools.partial(final_body, other),
            [shape(dims, F32) for dims in sizes],
            2 * depth * code,
            4 * depth * code,
            factors, core_arg, half_rows, *outs,
            smem=(0, 1),
            held=[(dims[0], dims[1] // 2) for dims in sizes],
            aliases={3 + i: i for i in range(len(outs))},
        )
    entry, exit_, blend = outs
    return state[None], entry, exit_, blend, observation_slope


def solution(mesh):
    placed = (
        P(BOTH, None),
        P(BOTH, None),
        P(BOTH, None),
        P(),
        P(),
        P(),
        P(BOTH, None),
        P(BOTH, None),
        P(),
        P(BOTH, None, None),
    )
    return jax.shard_map(
        shards,
        mesh=mesh,
        in_specs=placed,
        out_specs=(P(BOTH, None, None), P(), P(), P(), P(BOTH, None)),
        check_vma=False,
    )
```

```python
import functools
import math

import jax
import jax.numpy as jnp
import numpy as np
from jax import lax
from jax.experimental import pallas as pl
from jax.experimental.pallas import tpu as pltpu
from jax.sharding import PartitionSpec as P

LON = 1440
MODES = 128
CAP = 2
LANES = 128
BOTH = ("enc", "blk")
BF16 = jnp.bfloat16
F32 = jnp.float32
TILES = ((0, 384), (384, 384), (768, 384), (1152, 288))


def dot(a, b):
    return jnp.dot(a, b, preferred_element_type=F32)


def dot_ta(a, b):
    return lax.dot_general(a, b, (((0,), (0,)), ((), ())), preferred_element_type=F32)


def dot_tb(a, b):
    return lax.dot_general(a, b, (((1,), (1,)), ((), ())), preferred_element_type=F32)


def logistic(values):
    return 0.5 * jnp.tanh(0.5 * values) + 0.5


def local_kernel(body, out_shape, flops, moved, *operands, smem=(), room=6, held=(), aliases=None):
    vmem = pl.BlockSpec(memory_space=pltpu.VMEM)
    in_specs = [pl.BlockSpec(memory_space=pltpu.SMEM) if i in smem else vmem for i in range(len(operands))]
    single = not isinstance(out_shape, (tuple, list))
    far = pl.BlockSpec(memory_space=pl.ANY)
    aliases = aliases or {}
    in_specs = [far if i in aliases else spec for i, spec in enumerate(in_specs)]
    out = far if held else vmem
    return pl.pallas_call(
        body,
        out_shape=out_shape,
        in_specs=in_specs,
        out_specs=out if single else [out] * len(out_shape),
        scratch_shapes=[pltpu.VMEM(dims, F32) for dims in held] + ([pltpu.SemaphoreType.DMA((len(held),))] if held else []),
        input_output_aliases=aliases,
        compiler_params=pltpu.CompilerParams(vmem_limit_bytes=room * 1024 * 1024),
        cost_estimate=pl.CostEstimate(flops=flops, bytes_accessed=moved, transcendentals=0),
    )(*operands)


def shape(dims, dtype):
    return jax.ShapeDtypeStruct(dims, dtype)


def split(index, size):
    assert size & (size - 1) == 0
    return index >> (size.bit_length() - 1), index & (size - 1)


def order_rows(slots, source):
    at = lax.broadcasted_iota(jnp.int32, (slots, 1), 0)
    return (source(at) == lax.broadcasted_iota(jnp.int32, (slots, slots), 1)).astype(BF16)


def mix_body(
    core, spectrum, inside, beyond, w_spec, north, south, w_mix, weight, table_t, table, cotangent,
    pair, coeffs_out, to_beyond, to_inside,
):
    first = core[0] == 0
    near_row = jnp.where(first, south[...], north[...])
    far_row = jnp.where(first, north[...], south[...])
    scale = weight[...]
    mix = (
        spectrum[...] * w_spec[...] + near_row * inside[...].astype(F32) + far_row * beyond[...].astype(F32)
    ).astype(BF16)
    pair[: mix.shape[0], :] = mix
    coeffs = (dot(mix, w_mix[...]) * scale).astype(BF16)
    coeffs_out[...] = coeffs
    total = jnp.zeros(spectrum.shape, F32)
    for low, size in TILES:
        part = pl.ds(low, size)
        pre_act = dot(table_t[part, :], coeffs)
        gate = logistic(pre_act)
        slope = gate * (1.0 + pre_act * (1.0 - gate))
        grad_pre = (cotangent[part, :].astype(F32) * slope).astype(BF16)
        total += dot(table[:, part], grad_pre)
    grad_coeffs = (total * scale).astype(BF16)
    pair[mix.shape[0] :, :] = grad_coeffs
    grad_mix = dot_tb(grad_coeffs, w_mix[...])
    to_beyond[...] = (far_row * grad_mix).astype(BF16)
    to_inside[...] = (near_row * grad_mix).astype(BF16)


def state_body(table_t, coeffs, onehot, latent, state):
    for low, size in TILES:
        part = pl.ds(low, size)
        pre_act = dot(table_t[part, :], coeffs[...])
        state[part, :] = (dot(onehot[part, :], latent[...]) + pre_act * logistic(pre_act)).astype(BF16)


def back_body(
    core, from_beyond, from_inside, share, pair, w_mix, w_spec, rows, w_in, slot_modes, slot_cot, w_out,
    sent, mine, kept,
):
    first = core[0] == 0
    count = pair.shape[0] // 2
    mix, coeffs = pair[:count, :], pair[count:, :]
    grad_mix = dot_tb(coeffs, w_mix[...])
    grad_spec = (w_spec[...] * grad_mix + from_inside[...].astype(F32) + from_beyond[...].astype(F32)).astype(BF16)
    pre1 = dot(rows[...], w_in[...])
    gate = logistic(pre1)
    hidden = (pre1 * gate).astype(BF16)
    slope = gate * (1.0 + pre1 * (1.0 - gate))
    from_modes = dot_ta(slot_modes[...], grad_spec)
    grad_latent = ((slot_cot[...].astype(F32) + from_modes) * share[...]).astype(BF16)
    grad_pre1 = (dot_tb(grad_latent, w_out[...]) * slope).astype(BF16)
    row_slope = dot_tb(grad_pre1, w_in[...]).astype(BF16)
    half = row_slope.shape[0] // 2

    def source(at):
        other, rest = split(at, half)
        block, slot = split(rest, CAP)
        return (block * 2 + ((other + core[0]) & 1)) * CAP + slot

    ordered = dot(order_rows(row_slope.shape[0], source), row_slope).astype(BF16)
    kept[...] = ordered[:half]
    sent[mine.shape[0] :, :] = ordered[half:]
    at = 0
    depth = mine.shape[0] // 2
    for left, right in ((hidden, grad_latent), (mix, coeffs), (rows[...], grad_pre1)):
        width = right.shape[1] // 2
        low, high = right[:, :width], right[:, width:]
        near = dot_ta(left, jnp.where(first, low, high))
        far = dot_ta(left, jnp.where(first, high, low)).astype(BF16)
        size = near.shape[0]
        for piece in range(2):
            lanes = slice(piece * LANES, (piece + 1) * LANES)
            mine[piece * depth + at : piece * depth + at + size, :] = near[:, lanes]
            sent[piece * depth + at : piece * depth + at + size, :] = far[:, lanes]
        at += size


def scatter_body(mine, kept, got, out):
    count = out.shape[0]
    size = mine.shape[0] // count
    few = kept.shape[0] // count
    for i in range(count):
        out[i, :few, :] = kept[i * few : (i + 1) * few, :]
        out[i, few : 2 * few, :] = got[mine.shape[0] + i * few : mine.shape[0] + (i + 1) * few, :]
        part = slice(i * size, (i + 1) * size)
        out[i, 2 * few :, :] = (mine[part, :] + got[part, :].astype(F32)).astype(BF16)


def relay_body(slots, got, out):
    sources = got.shape[0]
    count = out.shape[0]
    few = slots // sources
    more = slots // count

    def source(at):
        z, rest = split(at, more)
        block, slot = split(rest, CAP)
        return (block * count + z) * CAP + slot

    total = got[0, few:, :].astype(F32)
    for i in range(1, sources):
        total += got[i, few:, :].astype(F32)
    total = total.astype(BF16)
    ordered = dot(order_rows(slots, source), jnp.concatenate([got[i, :few, :] for i in range(sources)], 0)).astype(BF16)
    for i in range(count):
        out[i, :more, :] = ordered[i * more : (i + 1) * more, :]
        out[i, more:, :] = total


def spread_body(few, got, out):
    total = got[0, few:, :].astype(F32)
    for i in range(1, got.shape[0]):
        total += got[i, few:, :].astype(F32)
    total = total.astype(BF16)
    for i in range(out.shape[0]):
        out[i, :, :] = total


def return_body(encs, core, got, slope):
    sources = got.shape[0]
    slots = slope.shape[0]
    few = slots // sources

    def source(at):
        enc, rest = split(at, slots // encs)
        z, rest = split(rest, 2 * CAP)
        which, slot = split(rest, CAP)
        return ((z * encs + enc) * 2 + ((which + core[0]) & 1)) * CAP + slot

    ordered = dot(order_rows(slots, source), jnp.concatenate([got[i, :few, :] for i in range(sources)], 0))
    slope[...] = ordered.astype(BF16)


def final_body(other, factors, core, half, *refs):
    outs, held, sems = refs[-7:-4], refs[-4:-1], refs[-1]
    side = (core[0] + 1) & 1 if other else core[0]
    width = held[0].shape[1]
    pieces = width // LANES
    depth = half.shape[0] // pieces
    at = 0
    copies = []
    for i, index in enumerate((1, 2, 0)):
        size = held[index].shape[0]
        for piece in range(pieces):
            part = slice(piece * depth + at, piece * depth + at + size)
            held[index][:, piece * LANES : (piece + 1) * LANES] = half[part, :].astype(F32) * factors[i & 1]
        at += size
        target = outs[index].at[:, pl.ds(pl.multiple_of(side * width, width), width)]
        copies.append(pltpu.make_async_copy(held[index], target, sems.at[index]))
        copies[-1].start()
    for copy in copies:
        copy.wait()


def phase_tables():
    product = np.arange(MODES)[:, None] * np.arange(LON)[None, :] % LON
    phases = product.astype(np.float64) * (2.0 * math.pi / LON)
    table = np.concatenate([np.cos(phases), -np.sin(phases)], 0)
    return jnp.asarray(table, BF16), jnp.asarray(np.ascontiguousarray(table.T), BF16)


def trade(near, far, count):
    links = [(i, i + 1) for i in range(1, count - 1, 2)]
    beyond = lax.ppermute(far, BOTH, links + [(j, i) for i, j in links])
    inside = lax.ppermute(near, BOTH, [(i, i ^ 1) for i in range(count)])
    return inside, beyond


def all_swap(blocks, axis, groups=None):
    return lax.all_to_all(blocks, axis, split_axis=0, concat_axis=0, tiled=True, axis_index_groups=groups)


def shards(
    observations, lon_index, live_count, w_in, w_out, w_spec, north, south, w_mix, loss_sensitivity
):
    encs = lax.axis_size("enc")
    blks = lax.axis_size("blk")
    deep = blks // 2
    devices = encs * blks
    slots, channels = observations.shape
    hid, code = w_out.shape
    core = lax.axis_index("blk") % 2
    core_arg = core.astype(jnp.int32).reshape(1)
    swap = [(j, j ^ 1) for j in range(blks)]
    columns = [[2 * i + k for i in range(deep)] for k in range(2)]

    rows = all_swap(observations.reshape(devices, CAP, channels), BOTH).reshape(slots, channels)

    lon = lon_index[0]
    live = (jnp.arange(CAP, dtype=jnp.int32)[None, :] < live_count[0][:, None]).reshape(-1)
    cell, core_arg = lax.optimization_barrier((jnp.where(live, lon, -1), core_arg))
    shared = jnp.sum((lon[:, None] == cell[None, :]).astype(F32), axis=1)
    share = (1.0 / jnp.maximum(shared, 1.0))[:, None]
    table, table_t = phase_tables()
    weight = jnp.asarray(np.where(np.arange(2 * MODES) % MODES == 0, 1.0, 2.0)[:, None] / LON, F32)
    cotangent = loss_sensitivity[0]
    half = slots // 2
    modes = (2 * MODES, code)
    onehot = (cell[None, :] == jnp.arange(LON, dtype=jnp.int32)[:, None]).astype(BF16)
    slot_modes = dot(table, onehot).astype(BF16)
    slot_cot = dot_ta(onehot, cotangent).astype(BF16)
    pre1 = dot(rows, w_in)
    hidden = (pre1 * logistic(pre1)).astype(BF16)
    latent = (dot(hidden, w_out) * share).astype(BF16)
    spectrum = dot(slot_modes, latent)
    outgoing = spectrum.astype(BF16)
    inside, beyond = trade(outgoing, outgoing, devices)

    pair, coeffs, to_beyond, to_inside = local_kernel(
        mix_body,
        [shape((4 * MODES, code), BF16), shape(modes, BF16), shape(modes, BF16), shape(modes, BF16)],
        2 * LON * code * 4 * MODES,
        6 * LON * code,
        core_arg, spectrum, inside, beyond, w_spec, north, south, w_mix, weight, table_t, table, cotangent,
        smem=(0,),
        room=12,
    )
    state = local_kernel(
        state_body,
        shape((LON, code), BF16),
        2 * LON * code * (2 * MODES + slots),
        6 * LON * code,
        table_t, coeffs, onehot, latent,
        room=8,
    )
    from_inside, from_beyond = trade(to_inside, to_beyond, devices)
    state, pair = lax.optimization_barrier((state, pair))
    depth = hid + code + channels
    sent, mine, kept = local_kernel(
        back_body,
        [shape((2 * depth + half, LANES), BF16), shape((2 * depth, LANES), F32), shape((half, LANES), BF16)],
        2 * slots * code * 1500,
        6 * slots * code,
        core_arg, from_beyond, from_inside, share, pair, w_mix, w_spec, rows, w_in, slot_modes, slot_cot, w_out,
        smem=(0,),
        room=12,
    )
    got = lax.ppermute(sent, "blk", swap)
    chunk = 2 * depth // encs
    few, more = slots // encs, slots // deep
    parts = local_kernel(
        scatter_body, shape((encs, few + chunk, LANES), BF16), depth * LANES, 16 * depth * LANES, mine, kept, got
    )
    parts = all_swap(parts, "enc")
    parts = local_kernel(
        functools.partial(relay_body, slots),
        shape((deep, more + chunk, LANES), BF16),
        10 * depth * LANES,
        8 * depth * LANES,
        parts,
    )
    parts = all_swap(parts, "blk", columns)
    spread = local_kernel(
        functools.partial(spread_body, more), shape((encs, chunk, LANES), BF16), 10 * depth * LANES, 8 * depth * LANES, parts
    )
    observation_slope = local_kernel(
        functools.partial(return_body, encs),
        shape((slots, LANES), BF16),
        2 * slots * slots * LANES,
        4 * slots * LANES,
        core_arg, parts,
        smem=(0,),
    )
    whole = all_swap(spread, "enc").reshape(2 * depth, LANES)
    theirs = lax.ppermute(whole, "blk", swap)
    factors = jnp.array([1.0 / math.sqrt(devices * slots), 1.0 / math.sqrt(devices * LON)], F32)
    sizes = ((channels, hid), (hid, code), (code, code))
    outs = []
    for other, half_rows in ((False, whole), (True, theirs)):
        outs = local_kernel(
            functools.partial(final_body, other),
            [shape(dims, F32) for dims in sizes],
            2 * depth * code,
            4 * depth * code,
            factors, core_arg, half_rows, *outs,
            smem=(0, 1),
            held=[(dims[0], dims[1] // 2) for dims in sizes],
            aliases={3 + i: i for i in range(len(outs))},
        )
    entry, exit_, blend = outs
    return state[None], entry, exit_, blend, observation_slope


def solution(mesh):
    placed = (
        P(BOTH, None),
        P(BOTH, None),
        P(BOTH, None),
        P(),
        P(),
        P(),
        P(BOTH, None),
        P(BOTH, None),
        P(),
        P(BOTH, None, None),
    )
    return jax.shard_map(
        shards,
        mesh=mesh,
        in_specs=placed,
        out_specs=(P(BOTH, None, None), P(), P(), P(), P(BOTH, None)),
        check_vma=False,
    )
```

```python
import functools
import math

import jax
import jax.numpy as jnp
import numpy as np
from jax import lax
from jax.experimental import pallas as pl
from jax.experimental.pallas import tpu as pltpu
from jax.sharding import PartitionSpec as P

LON = 1440
MODES = 128
CAP = 2
LANES = 128
BOTH = ("enc", "blk")
BF16 = jnp.bfloat16
F32 = jnp.float32
TILES = ((0, 384), (384, 384), (768, 384), (1152, 288))


def dot(a, b):
    return jnp.dot(a, b, preferred_element_type=F32)


def dot_ta(a, b):
    return lax.dot_general(a, b, (((0,), (0,)), ((), ())), preferred_element_type=F32)


def dot_tb(a, b):
    return lax.dot_general(a, b, (((1,), (1,)), ((), ())), preferred_element_type=F32)


def logistic(values):
    return 0.5 * jnp.tanh(0.5 * values) + 0.5


def local_kernel(body, out_shape, flops, moved, *operands, smem=(), room=6, held=(), aliases=None):
    vmem = pl.BlockSpec(memory_space=pltpu.VMEM)
    in_specs = [pl.BlockSpec(memory_space=pltpu.SMEM) if i in smem else vmem for i in range(len(operands))]
    single = not isinstance(out_shape, (tuple, list))
    far = pl.BlockSpec(memory_space=pl.ANY)
    aliases = aliases or {}
    in_specs = [far if i in aliases else spec for i, spec in enumerate(in_specs)]
    out = far if held else vmem
    return pl.pallas_call(
        body,
        out_shape=out_shape,
        in_specs=in_specs,
        out_specs=out if single else [out] * len(out_shape),
        scratch_shapes=[pltpu.VMEM(dims, F32) for dims in held] + ([pltpu.SemaphoreType.DMA((len(held),))] if held else []),
        input_output_aliases=aliases,
        compiler_params=pltpu.CompilerParams(vmem_limit_bytes=room * 1024 * 1024),
        cost_estimate=pl.CostEstimate(flops=flops, bytes_accessed=moved, transcendentals=0),
    )(*operands)


def shape(dims, dtype):
    return jax.ShapeDtypeStruct(dims, dtype)


def split(index, size):
    assert size & (size - 1) == 0
    return index >> (size.bit_length() - 1), index & (size - 1)


def order_rows(slots, source):
    at = lax.broadcasted_iota(jnp.int32, (slots, 1), 0)
    return (source(at) == lax.broadcasted_iota(jnp.int32, (slots, slots), 1)).astype(BF16)


def mix_body(
    core, spectrum, inside, beyond, w_spec, north, south, w_mix, weight, table_t, table, cotangent,
    pair, coeffs_out, to_beyond, to_inside,
):
    first = core[0] == 0
    near_row = jnp.where(first, south[...], north[...])
    far_row = jnp.where(first, north[...], south[...])
    scale = weight[...]
    mix = (
        spectrum[...] * w_spec[...] + near_row * inside[...].astype(F32) + far_row * beyond[...].astype(F32)
    ).astype(BF16)
    pair[: mix.shape[0], :] = mix
    coeffs = (dot(mix, w_mix[...]) * scale).astype(BF16)
    coeffs_out[...] = coeffs
    total = jnp.zeros(spectrum.shape, F32)
    for low, size in TILES:
        part = pl.ds(low, size)
        pre_act = dot(table_t[part, :], coeffs)
        gate = logistic(pre_act)
        slope = gate * (1.0 + pre_act * (1.0 - gate))
        grad_pre = (cotangent[part, :].astype(F32) * slope).astype(BF16)
        total += dot(table[:, part], grad_pre)
    grad_coeffs = (total * scale).astype(BF16)
    pair[mix.shape[0] :, :] = grad_coeffs
    grad_mix = dot_tb(grad_coeffs, w_mix[...])
    to_beyond[...] = (far_row * grad_mix).astype(BF16)
    to_inside[...] = (near_row * grad_mix).astype(BF16)


def state_body(table_t, coeffs, onehot, latent, state):
    for low, size in TILES:
        part = pl.ds(low, size)
        pre_act = dot(table_t[part, :], coeffs[...])
        state[part, :] = (dot(onehot[part, :], latent[...]) + pre_act * logistic(pre_act)).astype(BF16)


def back_body(
    core, from_beyond, from_inside, share, pair, w_mix, w_spec, rows, w_in, slot_modes, slot_cot, w_out,
    sent, mine, kept,
):
    first = core[0] == 0
    count = pair.shape[0] // 2
    mix, coeffs = pair[:count, :], pair[count:, :]
    grad_mix = dot_tb(coeffs, w_mix[...])
    grad_spec = (w_spec[...] * grad_mix + from_inside[...].astype(F32) + from_beyond[...].astype(F32)).astype(BF16)
    pre1 = dot(rows[...], w_in[...])
    gate = logistic(pre1)
    hidden = (pre1 * gate).astype(BF16)
    slope = gate * (1.0 + pre1 * (1.0 - gate))
    from_modes = dot_ta(slot_modes[...], grad_spec)
    grad_latent = ((slot_cot[...].astype(F32) + from_modes) * share[...]).astype(BF16)
    grad_pre1 = (dot_tb(grad_latent, w_out[...]) * slope).astype(BF16)
    row_slope = dot_tb(grad_pre1, w_in[...]).astype(BF16)
    half = row_slope.shape[0] // 2

    def source(at):
        other, rest = split(at, half)
        block, slot = split(rest, CAP)
        return (block * 2 + ((other + core[0]) & 1)) * CAP + slot

    ordered = dot(order_rows(row_slope.shape[0], source), row_slope).astype(BF16)
    kept[...] = ordered[:half]
    sent[mine.shape[0] :, :] = ordered[half:]
    at = 0
    depth = mine.shape[0] // 2
    for left, right in ((hidden, grad_latent), (mix, coeffs), (rows[...], grad_pre1)):
        width = right.shape[1] // 2
        low, high = right[:, :width], right[:, width:]
        near = dot_ta(left, jnp.where(first, low, high))
        far = dot_ta(left, jnp.where(first, high, low)).astype(BF16)
        size = near.shape[0]
        for piece in range(2):
            lanes = slice(piece * LANES, (piece + 1) * LANES)
            mine[piece * depth + at : piece * depth + at + size, :] = near[:, lanes]
            sent[piece * depth + at : piece * depth + at + size, :] = far[:, lanes]
        at += size


def scatter_body(mine, kept, got, out):
    count = out.shape[0]
    size = mine.shape[0] // count
    few = kept.shape[0] // count
    for i in range(count):
        out[i, :few, :] = kept[i * few : (i + 1) * few, :]
        out[i, few : 2 * few, :] = got[mine.shape[0] + i * few : mine.shape[0] + (i + 1) * few, :]
        part = slice(i * size, (i + 1) * size)
        out[i, 2 * few :, :] = (mine[part, :] + got[part, :].astype(F32)).astype(BF16)


def relay_body(slots, got, out):
    sources = got.shape[0]
    count = out.shape[0]
    few = slots // sources
    more = slots // count

    def source(at):
        z, rest = split(at, more)
        block, slot = split(rest, CAP)
        return (block * count + z) * CAP + slot

    total = got[0, few:, :].astype(F32)
    for i in range(1, sources):
        total += got[i, few:, :].astype(F32)
    total = total.astype(BF16)
    ordered = dot(order_rows(slots, source), jnp.concatenate([got[i, :few, :] for i in range(sources)], 0)).astype(BF16)
    for i in range(count):
        out[i, :more, :] = ordered[i * more : (i + 1) * more, :]
        out[i, more:, :] = total


def spread_body(few, got, out):
    total = got[0, few:, :].astype(F32)
    for i in range(1, got.shape[0]):
        total += got[i, few:, :].astype(F32)
    total = total.astype(BF16)
    for i in range(out.shape[0]):
        out[i, :, :] = total


def return_body(encs, core, got, slope):
    sources = got.shape[0]
    slots = slope.shape[0]
    few = slots // sources

    def source(at):
        enc, rest = split(at, slots // encs)
        z, rest = split(rest, 2 * CAP)
        which, slot = split(rest, CAP)
        return ((z * encs + enc) * 2 + ((which + core[0]) & 1)) * CAP + slot

    ordered = dot(order_rows(slots, source), jnp.concatenate([got[i, :few, :] for i in range(sources)], 0))
    slope[...] = ordered.astype(BF16)


def final_body(other, factors, core, half, *refs):
    outs, held, sems = refs[-7:-4], refs[-4:-1], refs[-1]
    side = (core[0] + 1) & 1 if other else core[0]
    width = held[0].shape[1]
    pieces = width // LANES
    depth = half.shape[0] // pieces
    at = 0
    copies = []
    for i, index in enumerate((1, 2, 0)):
        size = held[index].shape[0]
        for piece in range(pieces):
            part = slice(piece * depth + at, piece * depth + at + size)
            held[index][:, piece * LANES : (piece + 1) * LANES] = half[part, :].astype(F32) * factors[i & 1]
        at += size
        target = outs[index].at[:, pl.ds(pl.multiple_of(side * width, width), width)]
        copies.append(pltpu.make_async_copy(held[index], target, sems.at[index]))
        copies[-1].start()
    for copy in copies:
        copy.wait()


def phase_tables():
    product = np.arange(MODES)[:, None] * np.arange(LON)[None, :] % LON
    phases = product.astype(np.float64) * (2.0 * math.pi / LON)
    table = np.concatenate([np.cos(phases), -np.sin(phases)], 0)
    return jnp.asarray(table, BF16), jnp.asarray(np.ascontiguousarray(table.T), BF16)


def trade(near, far, count):
    links = [(i, i + 1) for i in range(1, count - 1, 2)]
    beyond = lax.ppermute(far, BOTH, links + [(j, i) for i, j in links])
    inside = lax.ppermute(near, BOTH, [(i, i ^ 1) for i in range(count)])
    return inside, beyond


def all_swap(blocks, axis, groups=None):
    return lax.all_to_all(blocks, axis, split_axis=0, concat_axis=0, tiled=True, axis_index_groups=groups)


def shards(
    observations, lon_index, live_count, w_in, w_out, w_spec, north, south, w_mix, loss_sensitivity
):
    encs = lax.axis_size("enc")
    blks = lax.axis_size("blk")
    deep = blks // 2
    devices = encs * blks
    slots, channels = observations.shape
    hid, code = w_out.shape
    core = lax.axis_index("blk") % 2
    core_arg = core.astype(jnp.int32).reshape(1)
    swap = [(j, j ^ 1) for j in range(blks)]
    columns = [[2 * i + k for i in range(deep)] for k in range(2)]

    rows = all_swap(observations.reshape(devices, CAP, channels), BOTH).reshape(slots, channels)

    lon = lon_index[0]
    live = (jnp.arange(CAP, dtype=jnp.int32)[None, :] < live_count[0][:, None]).reshape(-1)
    cell, core_arg = lax.optimization_barrier((jnp.where(live, lon, -1), core_arg))
    shared = jnp.sum((lon[:, None] == cell[None, :]).astype(F32), axis=1)
    share = (1.0 / jnp.maximum(shared, 1.0))[:, None]
    table, table_t = phase_tables()
    weight = jnp.asarray(np.where(np.arange(2 * MODES) % MODES == 0, 1.0, 2.0)[:, None] / LON, F32)
    cotangent = loss_sensitivity[0]
    half = slots // 2
    modes = (2 * MODES, code)
    onehot = (cell[None, :] == jnp.arange(LON, dtype=jnp.int32)[:, None]).astype(BF16)
    slot_modes = dot(table, onehot).astype(BF16)
    slot_cot = dot_ta(onehot, cotangent).astype(BF16)
    pre1 = dot(rows, w_in)
    hidden = (pre1 * logistic(pre1)).astype(BF16)
    latent = (dot(hidden, w_out) * share).astype(BF16)
    spectrum = dot(slot_modes, latent)
    outgoing = spectrum.astype(BF16)
    inside, beyond = trade(outgoing, outgoing, devices)

    pair, coeffs, to_beyond, to_inside = local_kernel(
        mix_body,
        [shape((4 * MODES, code), BF16), shape(modes, BF16), shape(modes, BF16), shape(modes, BF16)],
        2 * LON * code * 4 * MODES,
        6 * LON * code,
        core_arg, spectrum, inside, beyond, w_spec, north, south, w_mix, weight, table_t, table, cotangent,
        smem=(0,),
        room=12,
    )
    state = local_kernel(
        state_body,
        shape((LON, code), BF16),
        2 * LON * code * (2 * MODES + slots),
        6 * LON * code,
        table_t, coeffs, onehot, latent,
        room=8,
    )
    from_inside, from_beyond = trade(to_inside, to_beyond, devices)
    state, pair = lax.optimization_barrier((state, pair))
    depth = hid + code + channels
    sent, mine, kept = local_kernel(
        back_body,
        [shape((2 * depth + half, LANES), BF16), shape((2 * depth, LANES), F32), shape((half, LANES), BF16)],
        2 * slots * code * 1500,
        6 * slots * code,
        core_arg, from_beyond, from_inside, share, pair, w_mix, w_spec, rows, w_in, slot_modes, slot_cot, w_out,
        smem=(0,),
        room=12,
    )
    got = lax.ppermute(sent, "blk", swap)
    chunk = 2 * depth // encs
    few, more = slots // encs, slots // deep
    parts = local_kernel(
        scatter_body, shape((encs, few + chunk, LANES), BF16), depth * LANES, 16 * depth * LANES, mine, kept, got
    )
    parts = all_swap(parts, "enc")
    parts = local_kernel(
        functools.partial(relay_body, slots),
        shape((deep, more + chunk, LANES), BF16),
        10 * depth * LANES,
        8 * depth * LANES,
        parts,
    )
    parts = all_swap(parts, "blk", columns)
    spread = local_kernel(
        functools.partial(spread_body, more), shape((encs, chunk, LANES), BF16), 10 * depth * LANES, 8 * depth * LANES, parts
    )
    observation_slope = local_kernel(
        functools.partial(return_body, encs),
        shape((slots, LANES), BF16),
        2 * slots * slots * LANES,
        4 * slots * LANES,
        core_arg, parts,
        smem=(0,),
    )
    whole = all_swap(spread, "enc").reshape(2 * depth, LANES)
    whole, observation_slope = lax.optimization_barrier((whole, observation_slope))
    theirs = lax.ppermute(whole, "blk", swap)
    factors = jnp.array([1.0 / math.sqrt(devices * slots), 1.0 / math.sqrt(devices * LON)], F32)
    sizes = ((channels, hid), (hid, code), (code, code))
    outs = []
    for other, half_rows in ((False, whole), (True, theirs)):
        outs = local_kernel(
            functools.partial(final_body, other),
            [shape(dims, F32) for dims in sizes],
            2 * depth * code,
            4 * depth * code,
            factors, core_arg, half_rows, *outs,
            smem=(0, 1),
            held=[(dims[0], dims[1] // 2) for dims in sizes],
            aliases={3 + i: i for i in range(len(outs))},
        )
    entry, exit_, blend = outs
    return state[None], entry, exit_, blend, observation_slope


def solution(mesh):
    placed = (
        P(BOTH, None),
        P(BOTH, None),
        P(BOTH, None),
        P(),
        P(),
        P(),
        P(BOTH, None),
        P(BOTH, None),
        P(),
        P(BOTH, None, None),
    )
    return jax.shard_map(
        shards,
        mesh=mesh,
        in_specs=placed,
        out_specs=(P(BOTH, None, None), P(), P(), P(), P(BOTH, None)),
        check_vma=False,
    )
```

```python
import functools
import math

import jax
import jax.numpy as jnp
import numpy as np
from jax import lax
from jax.experimental import pallas as pl
from jax.experimental.pallas import tpu as pltpu
from jax.sharding import PartitionSpec as P

LON = 1440
MODES = 128
CAP = 2
LANES = 128
BOTH = ("enc", "blk")
BF16 = jnp.bfloat16
F32 = jnp.float32
TILES = ((0, 384), (384, 384), (768, 384), (1152, 288))


def dot(a, b):
    return jnp.dot(a, b, preferred_element_type=F32)


def dot_ta(a, b):
    return lax.dot_general(a, b, (((0,), (0,)), ((), ())), preferred_element_type=F32)


def dot_tb(a, b):
    return lax.dot_general(a, b, (((1,), (1,)), ((), ())), preferred_element_type=F32)


def logistic(values):
    return 0.5 * jnp.tanh(0.5 * values) + 0.5


def local_kernel(body, out_shape, flops, moved, *operands, smem=(), room=6, held=(), aliases=None):
    vmem = pl.BlockSpec(memory_space=pltpu.VMEM)
    in_specs = [pl.BlockSpec(memory_space=pltpu.SMEM) if i in smem else vmem for i in range(len(operands))]
    single = not isinstance(out_shape, (tuple, list))
    far = pl.BlockSpec(memory_space=pl.ANY)
    aliases = aliases or {}
    in_specs = [far if i in aliases else spec for i, spec in enumerate(in_specs)]
    out = far if held else vmem
    return pl.pallas_call(
        body,
        out_shape=out_shape,
        in_specs=in_specs,
        out_specs=out if single else [out] * len(out_shape),
        scratch_shapes=[pltpu.VMEM(dims, F32) for dims in held] + ([pltpu.SemaphoreType.DMA((len(held),))] if held else []),
        input_output_aliases=aliases,
        compiler_params=pltpu.CompilerParams(vmem_limit_bytes=room * 1024 * 1024),
        cost_estimate=pl.CostEstimate(flops=flops, bytes_accessed=moved, transcendentals=0),
    )(*operands)


def shape(dims, dtype):
    return jax.ShapeDtypeStruct(dims, dtype)


def split(index, size):
    assert size & (size - 1) == 0
    return index >> (size.bit_length() - 1), index & (size - 1)


def order_rows(slots, source):
    at = lax.broadcasted_iota(jnp.int32, (slots, 1), 0)
    return (source(at) == lax.broadcasted_iota(jnp.int32, (slots, slots), 1)).astype(BF16)


def mix_body(
    core, spectrum, inside, beyond, w_spec, north, south, w_mix, weight, table_t, table, cotangent,
    pair, coeffs_out, to_beyond, to_inside,
):
    first = core[0] == 0
    near_row = jnp.where(first, south[...], north[...])
    far_row = jnp.where(first, north[...], south[...])
    scale = weight[...]
    mix = (
        spectrum[...] * w_spec[...] + near_row * inside[...].astype(F32) + far_row * beyond[...].astype(F32)
    ).astype(BF16)
    pair[: mix.shape[0], :] = mix
    coeffs = (dot(mix, w_mix[...]) * scale).astype(BF16)
    coeffs_out[...] = coeffs
    total = jnp.zeros(spectrum.shape, F32)
    for low, size in TILES:
        part = pl.ds(low, size)
        pre_act = dot(table_t[part, :], coeffs)
        gate = logistic(pre_act)
        slope = gate * (1.0 + pre_act * (1.0 - gate))
        grad_pre = (cotangent[part, :].astype(F32) * slope).astype(BF16)
        total += dot(table[:, part], grad_pre)
    grad_coeffs = (total * scale).astype(BF16)
    pair[mix.shape[0] :, :] = grad_coeffs
    grad_mix = dot_tb(grad_coeffs, w_mix[...])
    to_beyond[...] = (far_row * grad_mix).astype(BF16)
    to_inside[...] = (near_row * grad_mix).astype(BF16)


def halves(core, right):
    width = right.shape[1] // 2
    low, high = right[:, :width], right[:, width:]
    first = core[0] == 0
    return jnp.where(first, low, high), jnp.where(first, high, low)


def put(out, at, depth, value):
    for piece in range(value.shape[1] // LANES):
        start = piece * depth + at
        out[start : start + value.shape[0], :] = value[:, piece * LANES : (piece + 1) * LANES]


def state_body(core, table_t, coeffs, onehot, latent, pair, state, blend_near, blend_far):
    count = pair.shape[0] // 2
    near, far = halves(core, pair[count:, :])
    put(blend_near, 0, blend_near.shape[0] // 2, dot_ta(pair[:count, :], near))
    put(blend_far, 0, blend_far.shape[0] // 2, dot_ta(pair[:count, :], far).astype(BF16))
    for low, size in TILES:
        part = pl.ds(low, size)
        pre_act = dot(table_t[part, :], coeffs[...])
        state[part, :] = (dot(onehot[part, :], latent[...]) + pre_act * logistic(pre_act)).astype(BF16)


def back_body(
    core, from_beyond, from_inside, share, pair, w_mix, w_spec, rows, w_in, slot_modes, slot_cot, w_out,
    sent, mine, kept,
):
    count = pair.shape[0] // 2
    grad_mix = dot_tb(pair[count:, :], w_mix[...])
    grad_spec = (w_spec[...] * grad_mix + from_inside[...].astype(F32) + from_beyond[...].astype(F32)).astype(BF16)
    pre1 = dot(rows[...], w_in[...])
    gate = logistic(pre1)
    hidden = (pre1 * gate).astype(BF16)
    slope = gate * (1.0 + pre1 * (1.0 - gate))
    from_modes = dot_ta(slot_modes[...], grad_spec)
    grad_latent = ((slot_cot[...].astype(F32) + from_modes) * share[...]).astype(BF16)
    grad_pre1 = (dot_tb(grad_latent, w_out[...]) * slope).astype(BF16)
    row_slope = dot_tb(grad_pre1, w_in[...]).astype(BF16)
    half = row_slope.shape[0] // 2

    def source(at):
        other, rest = split(at, half)
        block, slot = split(rest, CAP)
        return (block * 2 + ((other + core[0]) & 1)) * CAP + slot

    ordered = dot(order_rows(row_slope.shape[0], source), row_slope).astype(BF16)
    kept[...] = ordered[:half]
    sent[mine.shape[0] :, :] = ordered[half:]
    at = 0
    depth = mine.shape[0] // 2
    for left, right in ((hidden, grad_latent), (rows[...], grad_pre1)):
        near, far = halves(core, right)
        put(mine, at, depth, dot_ta(left, near))
        put(sent, at, depth, dot_ta(left, far).astype(BF16))
        at += left.shape[1]


def scatter_body(mine, kept, got, blend_near, blend_got, out):
    count = out.shape[0]
    few = kept.shape[0] // count
    for i in range(count):
        out[i, :few, :] = kept[i * few : (i + 1) * few, :]
        out[i, few : 2 * few, :] = got[mine.shape[0] + i * few : mine.shape[0] + (i + 1) * few, :]
        at = 2 * few
        for ours, theirs in ((mine, got), (blend_near, blend_got)):
            size = ours.shape[0] // count
            part = slice(i * size, (i + 1) * size)
            out[i, at : at + size, :] = (ours[part, :] + theirs[part, :].astype(F32)).astype(BF16)
            at += size


def relay_body(slots, got, out):
    sources = got.shape[0]
    count = out.shape[0]
    few = slots // sources
    more = slots // count

    def source(at):
        z, rest = split(at, more)
        block, slot = split(rest, CAP)
        return (block * count + z) * CAP + slot

    total = got[0, few:, :].astype(F32)
    for i in range(1, sources):
        total += got[i, few:, :].astype(F32)
    total = total.astype(BF16)
    ordered = dot(order_rows(slots, source), jnp.concatenate([got[i, :few, :] for i in range(sources)], 0)).astype(BF16)
    for i in range(count):
        out[i, :more, :] = ordered[i * more : (i + 1) * more, :]
        out[i, more:, :] = total


def spread_body(few, got, out):
    total = got[0, few:, :].astype(F32)
    for i in range(1, got.shape[0]):
        total += got[i, few:, :].astype(F32)
    total = total.astype(BF16)
    for i in range(out.shape[0]):
        out[i, :, :] = total


def return_body(encs, core, got, slope):
    sources = got.shape[0]
    slots = slope.shape[0]
    few = slots // sources

    def source(at):
        enc, rest = split(at, slots // encs)
        z, rest = split(rest, 2 * CAP)
        which, slot = split(rest, CAP)
        return ((z * encs + enc) * 2 + ((which + core[0]) & 1)) * CAP + slot

    ordered = dot(order_rows(slots, source), jnp.concatenate([got[i, :few, :] for i in range(sources)], 0))
    slope[...] = ordered.astype(BF16)


def final_body(other, blocks, factors, core, half, *refs):
    outs, held, sems = refs[-7:-4], refs[-4:-1], refs[-1]
    entry, exit_, blend = held
    side = (core[0] + 1) & 1 if other else core[0]
    width = blend.shape[1]
    chunk = half.shape[0] // blocks
    late = 2 * blend.shape[0] // blocks
    early = chunk - late
    copies = []

    def send(index):
        target = outs[index].at[:, pl.ds(pl.multiple_of(side * width, width), width)]
        copies.append(pltpu.make_async_copy(held[index], target, sems.at[index]))
        copies[-1].start()

    for i in range(blocks):
        piece, at = divmod(i, blocks // 2)
        lanes = slice(piece * LANES, (piece + 1) * LANES)
        values = half[i * chunk + early : (i + 1) * chunk, :].astype(F32)
        blend[at * late : (at + 1) * late, lanes] = values * factors[1]
    send(2)
    for i in range(blocks):
        piece, at = divmod(i, blocks // 2)
        lanes = slice(piece * LANES, (piece + 1) * LANES)
        values = half[i * chunk : i * chunk + early, :].astype(F32) * factors[0]
        start, end = at * early, (at + 1) * early
        count = min(max(exit_.shape[0] - start, 0), early)
        if count:
            exit_[start : start + count, lanes] = values[:count]
        if count < early:
            entry[start + count - exit_.shape[0] : end - exit_.shape[0], lanes] = values[count:]
    send(1)
    send(0)
    for copy in copies:
        copy.wait()


def phase_tables():
    product = np.arange(MODES)[:, None] * np.arange(LON)[None, :] % LON
    phases = product.astype(np.float64) * (2.0 * math.pi / LON)
    table = np.concatenate([np.cos(phases), -np.sin(phases)], 0)
    return jnp.asarray(table, BF16), jnp.asarray(np.ascontiguousarray(table.T), BF16)


def trade(near, far, count):
    links = [(i, i + 1) for i in range(1, count - 1, 2)]
    beyond = lax.ppermute(far, BOTH, links + [(j, i) for i, j in links])
    inside = lax.ppermute(near, BOTH, [(i, i ^ 1) for i in range(count)])
    return inside, beyond


def all_swap(blocks, axis, groups=None):
    return lax.all_to_all(blocks, axis, split_axis=0, concat_axis=0, tiled=True, axis_index_groups=groups)


def shards(
    observations, lon_index, live_count, w_in, w_out, w_spec, north, south, w_mix, loss_sensitivity
):
    encs = lax.axis_size("enc")
    blks = lax.axis_size("blk")
    deep = blks // 2
    devices = encs * blks
    slots, channels = observations.shape
    hid, code = w_out.shape
    core = lax.axis_index("blk") % 2
    core_arg = core.astype(jnp.int32).reshape(1)
    swap = [(j, j ^ 1) for j in range(blks)]
    columns = [[2 * i + k for i in range(deep)] for k in range(2)]

    rows = all_swap(observations.reshape(devices, CAP, channels), BOTH).reshape(slots, channels)

    lon = lon_index[0]
    live = (jnp.arange(CAP, dtype=jnp.int32)[None, :] < live_count[0][:, None]).reshape(-1)
    cell, core_arg = lax.optimization_barrier((jnp.where(live, lon, -1), core_arg))
    shared = jnp.sum((lon[:, None] == cell[None, :]).astype(F32), axis=1)
    share = (1.0 / jnp.maximum(shared, 1.0))[:, None]
    table, table_t = phase_tables()
    weight = jnp.asarray(np.where(np.arange(2 * MODES) % MODES == 0, 1.0, 2.0)[:, None] / LON, F32)
    cotangent = loss_sensitivity[0]
    half = slots // 2
    modes = (2 * MODES, code)
    onehot = (cell[None, :] == jnp.arange(LON, dtype=jnp.int32)[:, None]).astype(BF16)
    slot_modes = dot(table, onehot).astype(BF16)
    slot_cot = dot_ta(onehot, cotangent).astype(BF16)
    pre1 = dot(rows, w_in)
    hidden = (pre1 * logistic(pre1)).astype(BF16)
    latent = (dot(hidden, w_out) * share).astype(BF16)
    spectrum = dot(slot_modes, latent)
    outgoing = spectrum.astype(BF16)
    inside, beyond = trade(outgoing, outgoing, devices)

    pair, coeffs, to_beyond, to_inside = local_kernel(
        mix_body,
        [shape((4 * MODES, code), BF16), shape(modes, BF16), shape(modes, BF16), shape(modes, BF16)],
        2 * LON * code * 4 * MODES,
        6 * LON * code,
        core_arg, spectrum, inside, beyond, w_spec, north, south, w_mix, weight, table_t, table, cotangent,
        smem=(0,),
        room=12,
    )
    state, blend_near, blend_far = local_kernel(
        state_body,
        [shape((LON, code), BF16), shape((2 * code, LANES), F32), shape((2 * code, LANES), BF16)],
        2 * LON * code * (2 * MODES + slots),
        6 * LON * code,
        core_arg, table_t, coeffs, onehot, latent, pair,
        smem=(0,),
        room=10,
    )
    from_inside, from_beyond = trade(to_inside, to_beyond, devices)
    blend_got = lax.ppermute(blend_far, "blk", swap)
    state, pair, blend_got = lax.optimization_barrier((state, pair, blend_got))
    depth = hid + channels
    sent, mine, kept = local_kernel(
        back_body,
        [shape((2 * depth + half, LANES), BF16), shape((2 * depth, LANES), F32), shape((half, LANES), BF16)],
        2 * slots * code * 1500,
        6 * slots * code,
        core_arg, from_beyond, from_inside, share, pair, w_mix, w_spec, rows, w_in, slot_modes, slot_cot, w_out,
        smem=(0,),
        room=12,
    )
    got = lax.ppermute(sent, "blk", swap)
    depth += code
    chunk = 2 * depth // encs
    few, more = slots // encs, slots // deep
    parts = local_kernel(
        scatter_body, shape((encs, few + chunk, LANES), BF16), depth * LANES, 16 * depth * LANES, mine, kept, got,
        blend_near, blend_got,
    )
    parts = all_swap(parts, "enc")
    parts = local_kernel(
        functools.partial(relay_body, slots),
        shape((deep, more + chunk, LANES), BF16),
        10 * depth * LANES,
        8 * depth * LANES,
        parts,
    )
    parts = all_swap(parts, "blk", columns)
    spread = local_kernel(
        functools.partial(spread_body, more), shape((encs, chunk, LANES), BF16), 10 * depth * LANES, 8 * depth * LANES, parts
    )
    observation_slope = local_kernel(
        functools.partial(return_body, encs),
        shape((slots, LANES), BF16),
        2 * slots * slots * LANES,
        4 * slots * LANES,
        core_arg, parts,
        smem=(0,),
    )
    whole = all_swap(spread, "enc").reshape(2 * depth, LANES)
    whole, observation_slope = lax.optimization_barrier((whole, observation_slope))
    theirs = lax.ppermute(whole, "blk", swap)
    factors = jnp.array([1.0 / math.sqrt(devices * slots), 1.0 / math.sqrt(devices * LON)], F32)
    sizes = ((channels, hid), (hid, code), (code, code))
    outs = []
    for other, half_rows in ((False, whole), (True, theirs)):
        outs = local_kernel(
            functools.partial(final_body, other, encs),
            [shape(dims, F32) for dims in sizes],
            2 * depth * code,
            4 * depth * code,
            factors, core_arg, half_rows, *outs,
            smem=(0, 1),
            held=[(dims[0], dims[1] // 2) for dims in sizes],
            aliases={3 + i: i for i in range(len(outs))},
        )
    entry, exit_, blend = outs
    return state[None], entry, exit_, blend, observation_slope


def solution(mesh):
    placed = (
        P(BOTH, None),
        P(BOTH, None),
        P(BOTH, None),
        P(),
        P(),
        P(),
        P(BOTH, None),
        P(BOTH, None),
        P(),
        P(BOTH, None, None),
    )
    return jax.shard_map(
        shards,
        mesh=mesh,
        in_specs=placed,
        out_specs=(P(BOTH, None, None), P(), P(), P(), P(BOTH, None)),
        check_vma=False,
    )
```

```python
import functools
import math

import jax
import jax.numpy as jnp
import numpy as np
from jax import lax
from jax.experimental import pallas as pl
from jax.experimental.pallas import tpu as pltpu
from jax.sharding import PartitionSpec as P

LON = 1440
MODES = 128
CAP = 2
LANES = 128
BOTH = ("enc", "blk")
BF16 = jnp.bfloat16
F32 = jnp.float32
TILES = ((0, 384), (384, 384), (768, 384), (1152, 288))


def dot(a, b):
    return jnp.dot(a, b, preferred_element_type=F32)


def dot_ta(a, b):
    return lax.dot_general(a, b, (((0,), (0,)), ((), ())), preferred_element_type=F32)


def dot_tb(a, b):
    return lax.dot_general(a, b, (((1,), (1,)), ((), ())), preferred_element_type=F32)


def logistic(values):
    return 0.5 * jnp.tanh(0.5 * values) + 0.5


def local_kernel(body, out_shape, flops, moved, *operands, smem=(), room=6, held=(), aliases=None):
    vmem = pl.BlockSpec(memory_space=pltpu.VMEM)
    in_specs = [pl.BlockSpec(memory_space=pltpu.SMEM) if i in smem else vmem for i in range(len(operands))]
    single = not isinstance(out_shape, (tuple, list))
    far = pl.BlockSpec(memory_space=pl.ANY)
    aliases = aliases or {}
    in_specs = [far if i in aliases else spec for i, spec in enumerate(in_specs)]
    out = far if held else vmem
    return pl.pallas_call(
        body,
        out_shape=out_shape,
        in_specs=in_specs,
        out_specs=out if single else [out] * len(out_shape),
        scratch_shapes=[pltpu.VMEM(dims, F32) for dims in held] + ([pltpu.SemaphoreType.DMA((len(held),))] if held else []),
        input_output_aliases=aliases,
        compiler_params=pltpu.CompilerParams(vmem_limit_bytes=room * 1024 * 1024),
        cost_estimate=pl.CostEstimate(flops=flops, bytes_accessed=moved, transcendentals=0),
    )(*operands)


def shape(dims, dtype):
    return jax.ShapeDtypeStruct(dims, dtype)


def split(index, size):
    assert size & (size - 1) == 0
    return index >> (size.bit_length() - 1), index & (size - 1)


def order_rows(slots, source):
    at = lax.broadcasted_iota(jnp.int32, (slots, 1), 0)
    return (source(at) == lax.broadcasted_iota(jnp.int32, (slots, slots), 1)).astype(BF16)


def mix_body(
    core, spectrum, inside, beyond, w_spec, north, south, w_mix, weight, table_t, table, cotangent,
    pair, coeffs_out, to_beyond, to_inside,
):
    first = core[0] == 0
    near_row = jnp.where(first, south[...], north[...])
    far_row = jnp.where(first, north[...], south[...])
    scale = weight[...]
    mix = (
        spectrum[...] * w_spec[...] + near_row * inside[...].astype(F32) + far_row * beyond[...].astype(F32)
    ).astype(BF16)
    pair[: mix.shape[0], :] = mix
    coeffs = (dot(mix, w_mix[...]) * scale).astype(BF16)
    coeffs_out[...] = coeffs
    total = jnp.zeros(spectrum.shape, F32)
    for low, size in TILES:
        part = pl.ds(low, size)
        pre_act = dot(table_t[part, :], coeffs)
        half = 0.5 * pre_act
        bend = jnp.tanh(half)
        slope = 1.0 + bend + half * (1.0 - bend * bend)
        grad_pre = (cotangent[part, :].astype(F32) * slope).astype(BF16)
        total += dot(table[:, part], grad_pre)
    grad_coeffs = (total * (0.5 * scale)).astype(BF16)
    pair[mix.shape[0] :, :] = grad_coeffs
    grad_mix = dot_tb(grad_coeffs, w_mix[...])
    to_beyond[...] = (far_row * grad_mix).astype(BF16)
    to_inside[...] = (near_row * grad_mix).astype(BF16)


def halves(core, right):
    width = right.shape[1] // 2
    low, high = right[:, :width], right[:, width:]
    first = core[0] == 0
    return jnp.where(first, low, high), jnp.where(first, high, low)


def put(out, at, depth, value):
    for piece in range(value.shape[1] // LANES):
        start = piece * depth + at
        out[start : start + value.shape[0], :] = value[:, piece * LANES : (piece + 1) * LANES]


def state_body(core, table_t, coeffs, onehot, latent, pair, state, blend_near, blend_far):
    count = pair.shape[0] // 2
    near, far = halves(core, pair[count:, :])
    put(blend_near, 0, blend_near.shape[0] // 2, dot_ta(pair[:count, :], near))
    put(blend_far, 0, blend_far.shape[0] // 2, dot_ta(pair[:count, :], far).astype(BF16))
    for low, size in TILES:
        part = pl.ds(low, size)
        pre_act = dot(table_t[part, :], coeffs[...])
        state[part, :] = (dot(onehot[part, :], latent[...]) + pre_act * logistic(pre_act)).astype(BF16)


def back_body(
    core, from_beyond, from_inside, share, pair, w_mix, w_spec, rows, w_in, slot_modes, slot_cot, w_out,
    sent, mine, kept,
):
    count = pair.shape[0] // 2
    grad_mix = dot_tb(pair[count:, :], w_mix[...])
    grad_spec = (w_spec[...] * grad_mix + from_inside[...].astype(F32) + from_beyond[...].astype(F32)).astype(BF16)
    pre1 = dot(rows[...], w_in[...])
    gate = logistic(pre1)
    hidden = (pre1 * gate).astype(BF16)
    slope = gate * (1.0 + pre1 * (1.0 - gate))
    from_modes = dot_ta(slot_modes[...], grad_spec)
    grad_latent = ((slot_cot[...].astype(F32) + from_modes) * share[...]).astype(BF16)
    grad_pre1 = (dot_tb(grad_latent, w_out[...]) * slope).astype(BF16)
    row_slope = dot_tb(grad_pre1, w_in[...]).astype(BF16)
    half = row_slope.shape[0] // 2

    def source(at):
        other, rest = split(at, half)
        block, slot = split(rest, CAP)
        return (block * 2 + ((other + core[0]) & 1)) * CAP + slot

    ordered = dot(order_rows(row_slope.shape[0], source), row_slope).astype(BF16)
    kept[...] = ordered[:half]
    sent[mine.shape[0] :, :] = ordered[half:]
    at = 0
    depth = mine.shape[0] // 2
    for left, right in ((hidden, grad_latent), (rows[...], grad_pre1)):
        near, far = halves(core, right)
        put(mine, at, depth, dot_ta(left, near))
        put(sent, at, depth, dot_ta(left, far).astype(BF16))
        at += left.shape[1]


def scatter_body(mine, kept, got, blend_near, blend_got, out):
    count = out.shape[0]
    few = kept.shape[0] // count
    for i in range(count):
        out[i, :few, :] = kept[i * few : (i + 1) * few, :]
        out[i, few : 2 * few, :] = got[mine.shape[0] + i * few : mine.shape[0] + (i + 1) * few, :]
        at = 2 * few
        for ours, theirs in ((mine, got), (blend_near, blend_got)):
            size = ours.shape[0] // count
            part = slice(i * size, (i + 1) * size)
            out[i, at : at + size, :] = (ours[part, :] + theirs[part, :].astype(F32)).astype(BF16)
            at += size


def relay_body(slots, got, out):
    sources = got.shape[0]
    count = out.shape[0]
    few = slots // sources
    more = slots // count

    def source(at):
        z, rest = split(at, more)
        block, slot = split(rest, CAP)
        return (block * count + z) * CAP + slot

    total = got[0, few:, :].astype(F32)
    for i in range(1, sources):
        total += got[i, few:, :].astype(F32)
    total = total.astype(BF16)
    ordered = dot(order_rows(slots, source), jnp.concatenate([got[i, :few, :] for i in range(sources)], 0)).astype(BF16)
    for i in range(count):
        out[i, :more, :] = ordered[i * more : (i + 1) * more, :]
        out[i, more:, :] = total


def spread_body(few, got, out):
    total = got[0, few:, :].astype(F32)
    for i in range(1, got.shape[0]):
        total += got[i, few:, :].astype(F32)
    total = total.astype(BF16)
    for i in range(out.shape[0]):
        out[i, :, :] = total


def return_body(encs, core, got, slope):
    sources = got.shape[0]
    slots = slope.shape[0]
    few = slots // sources

    def source(at):
        enc, rest = split(at, slots // encs)
        z, rest = split(rest, 2 * CAP)
        which, slot = split(rest, CAP)
        return ((z * encs + enc) * 2 + ((which + core[0]) & 1)) * CAP + slot

    ordered = dot(order_rows(slots, source), jnp.concatenate([got[i, :few, :] for i in range(sources)], 0))
    slope[...] = ordered.astype(BF16)


def final_body(other, blocks, factors, core, half, *refs):
    outs, held, sems = refs[-7:-4], refs[-4:-1], refs[-1]
    entry, exit_, blend = held
    side = (core[0] + 1) & 1 if other else core[0]
    width = blend.shape[1]
    chunk = half.shape[0] // blocks
    late = 2 * blend.shape[0] // blocks
    early = chunk - late
    copies = []

    def send(index):
        target = outs[index].at[:, pl.ds(pl.multiple_of(side * width, width), width)]
        copies.append(pltpu.make_async_copy(held[index], target, sems.at[index]))
        copies[-1].start()

    for i in range(blocks):
        piece, at = divmod(i, blocks // 2)
        lanes = slice(piece * LANES, (piece + 1) * LANES)
        values = half[i * chunk + early : (i + 1) * chunk, :].astype(F32)
        blend[at * late : (at + 1) * late, lanes] = values * factors[1]
    send(2)
    for i in range(blocks):
        piece, at = divmod(i, blocks // 2)
        lanes = slice(piece * LANES, (piece + 1) * LANES)
        values = half[i * chunk : i * chunk + early, :].astype(F32) * factors[0]
        start, end = at * early, (at + 1) * early
        count = min(max(exit_.shape[0] - start, 0), early)
        if count:
            exit_[start : start + count, lanes] = values[:count]
        if count < early:
            entry[start + count - exit_.shape[0] : end - exit_.shape[0], lanes] = values[count:]
    send(1)
    send(0)
    for copy in copies:
        copy.wait()


def phase_tables():
    product = np.arange(MODES)[:, None] * np.arange(LON)[None, :] % LON
    phases = product.astype(np.float64) * (2.0 * math.pi / LON)
    table = np.concatenate([np.cos(phases), -np.sin(phases)], 0)
    return jnp.asarray(table, BF16), jnp.asarray(np.ascontiguousarray(table.T), BF16)


def trade(near, far, count):
    links = [(i, i + 1) for i in range(1, count - 1, 2)]
    beyond = lax.ppermute(far, BOTH, links + [(j, i) for i, j in links])
    inside = lax.ppermute(near, BOTH, [(i, i ^ 1) for i in range(count)])
    return inside, beyond


def all_swap(blocks, axis, groups=None):
    return lax.all_to_all(blocks, axis, split_axis=0, concat_axis=0, tiled=True, axis_index_groups=groups)


def shards(
    observations, lon_index, live_count, w_in, w_out, w_spec, north, south, w_mix, loss_sensitivity
):
    encs = lax.axis_size("enc")
    blks = lax.axis_size("blk")
    deep = blks // 2
    devices = encs * blks
    slots, channels = observations.shape
    hid, code = w_out.shape
    core = lax.axis_index("blk") % 2
    core_arg = core.astype(jnp.int32).reshape(1)
    swap = [(j, j ^ 1) for j in range(blks)]
    columns = [[2 * i + k for i in range(deep)] for k in range(2)]

    rows = all_swap(observations.reshape(devices, CAP, channels), BOTH).reshape(slots, channels)

    lon = lon_index[0]
    live = (jnp.arange(CAP, dtype=jnp.int32)[None, :] < live_count[0][:, None]).reshape(-1)
    cell, core_arg = lax.optimization_barrier((jnp.where(live, lon, -1), core_arg))
    shared = jnp.sum((lon[:, None] == cell[None, :]).astype(F32), axis=1)
    share = (1.0 / jnp.maximum(shared, 1.0))[:, None]
    table, table_t = phase_tables()
    weight = jnp.asarray(np.where(np.arange(2 * MODES) % MODES == 0, 1.0, 2.0)[:, None] / LON, F32)
    cotangent = loss_sensitivity[0]
    half = slots // 2
    modes = (2 * MODES, code)
    onehot = (cell[None, :] == jnp.arange(LON, dtype=jnp.int32)[:, None]).astype(BF16)
    slot_modes = dot(table, onehot).astype(BF16)
    slot_cot = dot_ta(onehot, cotangent).astype(BF16)
    pre1 = dot(rows, w_in)
    hidden = (pre1 * logistic(pre1)).astype(BF16)
    latent = (dot(hidden, w_out) * share).astype(BF16)
    spectrum = dot(slot_modes, latent)
    outgoing = spectrum.astype(BF16)
    inside, beyond = trade(outgoing, outgoing, devices)

    pair, coeffs, to_beyond, to_inside = local_kernel(
        mix_body,
        [shape((4 * MODES, code), BF16), shape(modes, BF16), shape(modes, BF16), shape(modes, BF16)],
        2 * LON * code * 4 * MODES,
        6 * LON * code,
        core_arg, spectrum, inside, beyond, w_spec, north, south, w_mix, weight, table_t, table, cotangent,
        smem=(0,),
        room=12,
    )
    state, blend_near, blend_far = local_kernel(
        state_body,
        [shape((LON, code), BF16), shape((2 * code, LANES), F32), shape((2 * code, LANES), BF16)],
        2 * LON * code * (2 * MODES + slots),
        6 * LON * code,
        core_arg, table_t, coeffs, onehot, latent, pair,
        smem=(0,),
        room=10,
    )
    from_inside, from_beyond = trade(to_inside, to_beyond, devices)
    blend_got = lax.ppermute(blend_far, "blk", swap)
    state, pair, blend_got = lax.optimization_barrier((state, pair, blend_got))
    depth = hid + channels
    sent, mine, kept = local_kernel(
        back_body,
        [shape((2 * depth + half, LANES), BF16), shape((2 * depth, LANES), F32), shape((half, LANES), BF16)],
        2 * slots * code * 1500,
        6 * slots * code,
        core_arg, from_beyond, from_inside, share, pair, w_mix, w_spec, rows, w_in, slot_modes, slot_cot, w_out,
        smem=(0,),
        room=12,
    )
    got = lax.ppermute(sent, "blk", swap)
    depth += code
    chunk = 2 * depth // encs
    few, more = slots // encs, slots // deep
    parts = local_kernel(
        scatter_body, shape((encs, few + chunk, LANES), BF16), depth * LANES, 16 * depth * LANES, mine, kept, got,
        blend_near, blend_got,
    )
    parts = all_swap(parts, "enc")
    parts = local_kernel(
        functools.partial(relay_body, slots),
        shape((deep, more + chunk, LANES), BF16),
        10 * depth * LANES,
        8 * depth * LANES,
        parts,
    )
    parts = all_swap(parts, "blk", columns)
    spread = local_kernel(
        functools.partial(spread_body, more), shape((encs, chunk, LANES), BF16), 10 * depth * LANES, 8 * depth * LANES, parts
    )
    observation_slope = local_kernel(
        functools.partial(return_body, encs),
        shape((slots, LANES), BF16),
        2 * slots * slots * LANES,
        4 * slots * LANES,
        core_arg, parts,
        smem=(0,),
    )
    whole = all_swap(spread, "enc").reshape(2 * depth, LANES)
    whole, observation_slope = lax.optimization_barrier((whole, observation_slope))
    theirs = lax.ppermute(whole, "blk", swap)
    factors = jnp.array([1.0 / math.sqrt(devices * slots), 1.0 / math.sqrt(devices * LON)], F32)
    sizes = ((channels, hid), (hid, code), (code, code))
    outs = []
    for other, half_rows in ((False, whole), (True, theirs)):
        outs = local_kernel(
            functools.partial(final_body, other, encs),
            [shape(dims, F32) for dims in sizes],
            2 * depth * code,
            4 * depth * code,
            factors, core_arg, half_rows, *outs,
            smem=(0, 1),
            held=[(dims[0], dims[1] // 2) for dims in sizes],
            aliases={3 + i: i for i in range(len(outs))},
        )
    entry, exit_, blend = outs
    return state[None], entry, exit_, blend, observation_slope


def solution(mesh):
    placed = (
        P(BOTH, None),
        P(BOTH, None),
        P(BOTH, None),
        P(),
        P(),
        P(),
        P(BOTH, None),
        P(BOTH, None),
        P(),
        P(BOTH, None, None),
    )
    return jax.shard_map(
        shards,
        mesh=mesh,
        in_specs=placed,
        out_specs=(P(BOTH, None, None), P(), P(), P(), P(BOTH, None)),
        check_vma=False,
    )
```
